256 devices in a mesh: ctx: 16 (over y, z_hi, core), kv: 16 (over z_lo, x).
Axes of the slice: x: 4, y: 4, z: 8 (z_hi: 2, z_lo: 4; z = z_hi * 4 + z_lo), core: 2. Of those that a mesh axis runs over, the one named last changes fastest.
Arguments:
- queries: bfloat16 [2, 3072, 8192], P(None, 'ctx', 'kv'), may hold values from -112 to 112
- key_heads: bfloat16 [3072, 1024], P('ctx'), may hold values from -14 to 14
- value_heads: bfloat16 [3072, 1024], P('ctx'), may hold values from -6 to 6
- grad_out: bfloat16 [2, 3072, 8192], P(None, 'ctx', 'kv'), may hold values from -6 to 6
- offsets: int32 [32], replicated, may hold values from 0 to 2976, as said below
Outputs:
- grad_queries: bfloat16 [2, 3072, 8192], P(None, 'ctx', 'kv')
- grad_keys: float32 [3072, 1024], P('ctx')
- grad_values: float32 [3072, 1024], P('ctx')
The draws below stay inside these ranges and needn't reach their ends.
Inputs may be any that keep to these rules, and one draw needn't show every extreme that they name: `offsets`: each entry is a multiple of 96; every multiple below 3072 appears once; entries 2 c and 2 c + 1 sum to 2976.
All inputs are finite; a program needn't handle non-finite values.
Results may differ from the reference program's by a relative error of at most 0.0051.
Values may be sent and summed in bfloat16 or wider, within the bound.
A program may use at most 64 MiB of HBM per device.

```python
import math
import jax
import jax.numpy as jnp
from jax import lax

QH = 64
KVH = 8
HD = 128
LAYERS = 2
TOK_DEV = 192
TOKENS = 3072


def shared_keys(key, spread):
    raw_keys = jax.random.truncated_normal(key, -4.5, 4.5, (TOKENS, KVH, HD), jnp.float32)
    token_idx = jnp.arange(TOKENS, dtype=jnp.int32)
    chosen = token_idx % 64 == 33
    before = token_idx % 64 == 32
    scales = jnp.exp(jax.random.uniform(jax.random.fold_in(key, 1), (TOKENS,), jnp.float32) * math.log(spread))
    scales = jnp.where(chosen | before, 1.0, scales)
    keyed = raw_keys * scales[:, None, None]
    blended = keyed
    mixed = jnp.where(before[:, None, None], blended, keyed)
    return (mixed, chosen.astype(jnp.float32))


def draw_key_heads(key, part):
    spread = 1.0
    mixed, chosen = shared_keys(key, spread)
    return mixed.reshape(TOKENS, KVH * HD).astype(jnp.bfloat16)


def draw_queries(key, part):
    spread, strength = (1.0, 0.0)
    mixed, chosen = shared_keys(key, spread)
    key = jax.random.fold_in(key, 3)
    base = jax.random.truncated_normal(key, -4.5, 4.5, (LAYERS, TOKENS, QH, HD), jnp.float32)
    select = chosen[None, :, None, None] * strength
    mixed_q = base * (1.0 - select)
    return mixed_q.reshape(LAYERS, TOKENS, QH * HD).astype(jnp.bfloat16)


def draw_offsets(key, part):
    key = jax.random.fold_in(key, 5)
    shard_count = TOKENS // TOK_DEV
    order = jax.random.permutation(jax.random.fold_in(key, 1), shard_count)
    flips = jax.random.randint(jax.random.fold_in(key, 2), (shard_count,), 0, 2)
    first = jnp.where(flips == 0, order, 2 * shard_count - 1 - order)
    second = 2 * shard_count - 1 - first
    blocks = jnp.stack([first, second], axis=1).reshape(-1)
    return (blocks * (TOK_DEV // 2)).astype(jnp.int32)


def levels(own_key, extent, pieces, smallest, high):
    loudness, own = 1.0, jax.random.fold_in(own_key, 6)
    for position, blocks in pieces:
        draws = jnp.exp(jax.random.uniform(jax.random.fold_in(own, position), (blocks,), jnp.float32, smallest / len(pieces), high / len(pieces)))
        loudness = loudness * jnp.repeat(draws, extent[position] // blocks).reshape([-1 if axis == position else 1 for axis in range(len(extent))])
    return loudness


def normal_values(stream_key, extent, deviation, most, cuts=(), kind=jnp.bfloat16):
    loudness = levels(stream_key, extent, cuts, -0.22, 0.18) if cuts else 1.0
    drawn = jax.random.normal(stream_key, extent, jnp.float32) * deviation * loudness
    return jnp.minimum(jnp.maximum(drawn, -most), most).astype(kind)


def setup_inputs(seed: int = 0) -> dict:
    key_of = jax.random.split(jax.random.key(seed), 6)
    return {
        "queries": draw_queries(jax.random.fold_in(key_of[5], 71), 0),
        "key_heads": draw_key_heads(jax.random.fold_in(key_of[5], 71), 0),
        "value_heads": normal_values(key_of[2], (TOKENS, KVH * HD), 1.0, 6.0, ((0, 16),)),
        "grad_out": normal_values(key_of[3], (LAYERS, TOKENS, QH * HD), 1.0, 6.0, ((1, 16), (2, 16))),
        "offsets": draw_offsets(jax.random.fold_in(key_of[5], 71), 0),
    }


def token_positions(offsets):
    within = jnp.arange(TOK_DEV // 2, dtype=jnp.int32)
    return (offsets[:, None] + within[None, :]).reshape(-1).astype(jnp.int32)


def head_grads(query_head, out_grad, key_head, value_head, positions):
    scale_factor = HD ** -0.5
    visible = positions[None, :] <= positions[:, None]
    scores = jnp.dot(query_head, key_head.T, preferred_element_type=jnp.float32) * scale_factor
    scores = jnp.where(visible, scores, -1e30)
    row_max = jnp.max(scores, axis=1, keepdims=True)
    weights = jnp.exp(scores - row_max)
    probability = weights / jnp.sum(weights, axis=1, keepdims=True)
    probability_low = probability.astype(jnp.bfloat16)
    grad_prob = jnp.dot(out_grad, value_head.T, preferred_element_type=jnp.float32)
    row_delta = jnp.sum(probability * grad_prob, axis=1, keepdims=True)
    grad_scores = (probability * (grad_prob - row_delta)).astype(jnp.bfloat16)
    query_grad = jnp.dot(grad_scores, key_head, preferred_element_type=jnp.float32) * scale_factor
    key_grad = jnp.dot(grad_scores.T, query_head, preferred_element_type=jnp.float32) * scale_factor
    value_grad = jnp.dot(probability_low.T, out_grad, preferred_element_type=jnp.float32)
    return query_grad, key_grad, value_grad


def reference(queries, key_heads, value_heads, grad_out, offsets):
    positions = token_positions(offsets)
    group_size = QH // KVH
    query_all = queries.reshape(LAYERS, TOKENS, QH, HD)
    grad_all = grad_out.reshape(LAYERS, TOKENS, QH, HD)
    key_all = key_heads.reshape(TOKENS, KVH, HD)
    value_all = value_heads.reshape(TOKENS, KVH, HD)

    def per_group(group_idx):
        key_head = key_all[:, group_idx]
        value_head = value_all[:, group_idx]

        def per_item(running, item_idx):
            layer_idx = item_idx // group_size
            head_idx = group_idx * group_size + item_idx % group_size
            query_grad, key_grad, value_grad = head_grads(query_all[layer_idx, :, head_idx], grad_all[layer_idx, :, head_idx], key_head, value_head, positions)
            return (running[0] + key_grad, running[1] + value_grad), query_grad.astype(jnp.bfloat16)

        zero_init = jnp.zeros((TOKENS, HD), jnp.float32)
        (key_sum, value_sum), query_grads = lax.scan(per_item, (zero_init, zero_init), jnp.arange(LAYERS * group_size, dtype=jnp.int32))
        return key_sum, value_sum, query_grads

    key_sums, value_sums, query_grads = lax.map(per_group, jnp.arange(KVH, dtype=jnp.int32))
    shaped = query_grads.reshape(KVH, LAYERS, group_size, TOKENS, HD).transpose(1, 3, 0, 2, 4)
    grad_queries = shaped.reshape(LAYERS, TOKENS, QH * HD)
    grad_keys = key_sums.transpose(1, 0, 2).reshape(TOKENS, KVH * HD)
    grad_values = value_sums.transpose(1, 0, 2).reshape(TOKENS, KVH * HD)
    return grad_queries, grad_keys, grad_values
```

```python
import jax
import jax.numpy as jnp
from jax import lax
from jax.experimental import pallas as pl
from jax.experimental.pallas import tpu as pltpu
from jax.sharding import PartitionSpec as P

KVH = 8
HD = 128
TOK = 192
HALF = 96
CTX = 16
TOTAL = CTX * TOK
BLOCKS = 2 * CTX
LAYERS = 2
HEADS = 4
ROWS = LAYERS * HEADS * HALF
TILE = 384
TILE_BLOCKS = TILE // HALF
SCALE = HD ** -0.5
EXP2_SCALE = SCALE * 1.4426950408889634
MESH = pl.DeviceIdType.MESH
BF16 = jnp.bfloat16
F32 = jnp.float32


def place():
    ctx, kv = lax.axis_index("ctx"), lax.axis_index("kv")
    return ctx // 4, (ctx // 2) % 2, ctx % 2, kv // 4, kv % 4


def ctx_of(y, z_hi, core):
    return y * 4 + z_hi * 2 + core


def head_of(z_lo, x):
    return z_lo * 2 + x // 2


def gather_kernel(k_ref, v_ref, o_ref, own_sem, send_sem, y_sem, cross_sem, chip_sem):
    y, z_hi, core, z_lo, x = place()
    kv = z_lo * 4 + x
    me = ctx_of(y, z_hi, core)
    mate = ctx_of(y, z_hi, 1 - core)
    far = 1 - z_hi
    cross_from = jnp.where(z_lo < 2, 3, 0)
    at_low, at_high = z_lo == 0, z_lo == 3

    barrier = pltpu.get_barrier_semaphore()

    def greet(ctx, kv_idx):
        pl.semaphore_signal(barrier, inc=1, device_id=(ctx, kv_idx), device_id_type=MESH)

    for step in (1, 2, 3):
        greet(ctx_of((y + step) % 4, z_hi, core), kv)
    greet(mate, kv)
    greet(ctx_of(y, far, core), cross_from * 4 + x)
    pl.semaphore_wait(barrier, jnp.where(jnp.logical_or(at_low, at_high), 6, 4))

    def head_slice(ref, head):
        return ref.at[:, pl.ds(pl.multiple_of(head * HD, HD), HD)]

    def send_input(head, slot, ctx, kv_idx, send, recv):
        copies = []
        for part, ref in enumerate((k_ref, v_ref)):
            copies.append(pltpu.make_async_remote_copy(
                src_ref=head_slice(ref, head), dst_ref=o_ref.at[slot, part], send_sem=send.at[part],
                recv_sem=recv, device_id=(ctx, kv_idx), device_id_type=MESH))
        return copies

    def unit_wait(slot, sem):
        pltpu.make_async_copy(o_ref.at[slot], o_ref.at[slot], sem).wait()

    def cross(low, act):
        for nth in range(2):
            target = 2 + nth if low else nth
            for copy in send_input(head_of(target, x), me, ctx_of(y, far, core), target * 4 + x,
                                   send_sem.at[nth], cross_sem):
                act(copy)

    @pl.when(at_low)
    def _():
        cross(True, lambda copy: copy.start())

    @pl.when(at_high)
    def _():
        cross(False, lambda copy: copy.start())

    head = head_of(z_lo, x)
    own = [pltpu.make_async_copy(head_slice(ref, head), o_ref.at[me, part], own_sem.at[part])
           for part, ref in enumerate((k_ref, v_ref))]
    for copy in own:
        copy.start()
    pending = []
    for step in (2, 1, 3):
        copies = send_input(head, me, ctx_of((y + step) % 4, z_hi, core), kv, send_sem.at[1 + step], y_sem.at[0, step - 1])
        for copy in copies:
            copy.start()
        pending += copies
    to_mate = []

    def forward(slot):
        nth = len(to_mate)
        copy = pltpu.make_async_remote_copy(
            src_ref=o_ref.at[slot], dst_ref=o_ref.at[slot], send_sem=chip_sem.at[0, nth],
            recv_sem=chip_sem.at[1, nth], device_id=(mate, kv), device_id_type=MESH)
        copy.start()
        to_mate.append(copy)

    for copy in own:
        copy.wait()
    forward(me)
    across = ctx_of(y, far, core)
    unit_wait(across, cross_sem)
    onward = []
    for step in (2, 1, 3):
        copy = pltpu.make_async_remote_copy(
            src_ref=o_ref.at[across], dst_ref=o_ref.at[across], send_sem=send_sem.at[4 + step, 0],
            recv_sem=y_sem.at[1, step - 1], device_id=(ctx_of((y + step) % 4, z_hi, core), kv), device_id_type=MESH)
        copy.start()
        onward.append(copy)
    forward(across)
    for kind, half in ((0, z_hi), (1, far)):
        for step in (1, 3, 2):
            slot = ctx_of((y - step + 4) % 4, half, core)
            unit_wait(slot, y_sem.at[kind, step - 1])
            forward(slot)
    for copy in pending + onward:
        copy.wait_send()
    for copy in to_mate:
        copy.wait()

    @pl.when(at_low)
    def _():
        cross(True, lambda copy: copy.wait_send())

    @pl.when(at_high)
    def _():
        cross(False, lambda copy: copy.wait_send())


def gather_heads(key_heads, value_heads):
    dma = pltpu.SemaphoreType.DMA
    return pl.pallas_call(
        gather_kernel,
        out_shape=jax.ShapeDtypeStruct((CTX, 2, TOK, HD), BF16),
        in_specs=[pl.BlockSpec(memory_space=pl.ANY)] * 2,
        out_specs=pl.BlockSpec(memory_space=pl.ANY),
        scratch_shapes=[dma((2,)), dma((8, 2)), dma((2, 3)), dma, dma((2, 8))],
        compiler_params=pltpu.CompilerParams(collective_id=0, has_side_effects=True),
        name="gather_heads",
    )(key_heads, value_heads)


def compute_kernel(off_ref, q_ref, g_ref, kv_ref, dq_ref, part_ref, ks, vs, qs, gs, s_scr, p_scr, dq_acc, dk_acc, dv_acc, sem):
    ctx = lax.axis_index("ctx")
    nt_dims = (((1,), (1,)), ((), ()))
    tn_dims = (((0,), (0,)), ((), ()))

    def load(block, act):
        dst = pl.ds(pl.multiple_of(off_ref[block], HALF), HALF)
        rows = pl.ds((block % 2) * HALF, HALF)
        act(pltpu.make_async_copy(kv_ref.at[block // 2, 0, rows], ks.at[dst], sem.at[0]))
        act(pltpu.make_async_copy(kv_ref.at[block // 2, 1, rows], vs.at[dst], sem.at[1]))

    for block in range(BLOCKS):
        load(block, lambda copy: copy.start())
    dk_acc[...] = jnp.zeros_like(dk_acc)
    dv_acc[...] = jnp.zeros_like(dv_acc)
    for half in range(2):
        for layer in range(LAYERS):
            for head in range(HEADS):
                unit = layer * HEADS + head
                src = (layer, slice(half * HALF, (half + 1) * HALF), slice(head * HD, (head + 1) * HD))
                qs[half, unit * HALF:(unit + 1) * HALF] = q_ref[src]
                gs[half, unit * HALF:(unit + 1) * HALF] = g_ref[src]
    pltpu.make_async_copy(ks, ks, sem.at[0]).wait()
    pltpu.make_async_copy(vs, vs, sem.at[1]).wait()

    def fold(tile, op):
        return op(tile.reshape(TILE // 8, 8, ROWS), axis=0)

    def one_half(half, _):
        start = off_ref[2 * ctx + half]
        last = start // TILE
        q_t, g_t = qs[half], gs[half]

        def scores(tile):
            return lax.dot_general(ks[pl.ds(tile * TILE, TILE)], q_t, nt_dims, preferred_element_type=F32)

        def max_step(tile, top):
            s = scores(tile)
            s_scr[pl.ds(tile * TILE, TILE)] = s
            return jnp.maximum(top, fold(s, jnp.max))

        top = lax.fori_loop(0, last, max_step, jnp.full((8, ROWS), -1e30, F32))
        s = scores(last)
        key_idx = lax.broadcasted_iota(jnp.int32, (TILE, ROWS), 0) + last * TILE
        row_idx = lax.broadcasted_iota(jnp.int32, (TILE, ROWS), 1) % HALF + start
        s = jnp.where(key_idx <= row_idx, s, -1e30)
        s_scr[pl.ds(last * TILE, TILE)] = s
        top = jnp.max(jnp.maximum(top, fold(s, jnp.max)), axis=0, keepdims=True)

        def sum_step(tile, sums):
            rows = pl.ds(tile * TILE, TILE)
            weight = jnp.exp2((s_scr[rows] - top) * EXP2_SCALE)
            grad_prob = lax.dot_general(vs[rows], g_t, nt_dims, preferred_element_type=F32)
            s_scr[rows] = weight
            p_scr[rows] = grad_prob
            return sums[0] + fold(weight, jnp.sum), sums[1] + fold(weight * grad_prob, jnp.sum)

        zero = jnp.zeros((8, ROWS), F32)
        total, delta = lax.fori_loop(0, last + 1, sum_step, (zero, zero))
        inv = 1.0 / jnp.sum(total, axis=0, keepdims=True)
        delta = jnp.sum(delta, axis=0, keepdims=True) * inv
        dq_acc[...] = jnp.zeros_like(dq_acc)

        def grad_step(tile, _):
            rows = pl.ds(tile * TILE, TILE)
            prob = s_scr[rows] * inv
            grad_scores = (prob * (p_scr[rows] - delta)).astype(BF16)
            dv_acc[rows] += jnp.dot(prob.astype(BF16), g_t, preferred_element_type=F32)
            dk_acc[rows] += jnp.dot(grad_scores, q_t, preferred_element_type=F32)
            dq_acc[...] += lax.dot_general(grad_scores, ks[rows], tn_dims, preferred_element_type=F32)
            return 0

        lax.fori_loop(0, last + 1, grad_step, 0)
        for layer in range(LAYERS):
            for head in range(HEADS):
                unit = layer * HEADS + head
                dq_ref[layer, pl.ds(pl.multiple_of(half * HALF, HALF), HALF), head * HD:(head + 1) * HD] = (
                    dq_acc[unit * HALF:(unit + 1) * HALF] * SCALE).astype(BF16)
        return 0

    lax.fori_loop(0, 2, one_half, 0)
    for block in range(BLOCKS):
        src = pl.ds(pl.multiple_of(off_ref[block], HALF), HALF)
        dst = slice((block % 2) * HALF, (block % 2 + 1) * HALF)
        part_ref[block // 2, 0, dst] = (dk_acc[src] * SCALE).astype(BF16)
        part_ref[block // 2, 1, dst] = dv_acc[src].astype(BF16)


def compute(offsets, queries, grad_out, heads):
    vmem = pl.BlockSpec(memory_space=pltpu.VMEM)
    return pl.pallas_call(
        compute_kernel,
        out_shape=(jax.ShapeDtypeStruct(queries.shape, BF16), jax.ShapeDtypeStruct((CTX, 2, TOK, HD), BF16)),
        in_specs=[pl.BlockSpec(memory_space=pltpu.SMEM), vmem, vmem, pl.BlockSpec(memory_space=pl.ANY)],
        out_specs=(vmem, vmem),
        scratch_shapes=[
            pltpu.VMEM((TOTAL, HD), BF16), pltpu.VMEM((TOTAL, HD), BF16),
            pltpu.VMEM((2, ROWS, HD), BF16), pltpu.VMEM((2, ROWS, HD), BF16),
            pltpu.VMEM((TOTAL, ROWS), F32), pltpu.VMEM((TOTAL, ROWS), F32),
            pltpu.VMEM((ROWS, HD), F32), pltpu.VMEM((TOTAL, HD), F32), pltpu.VMEM((TOTAL, HD), F32),
            pltpu.SemaphoreType.DMA((2,)),
        ],
        compiler_params=pltpu.CompilerParams(vmem_limit_bytes=56 * 1024 * 1024),
        cost_estimate=pl.CostEstimate(flops=3_400_000_000, bytes_accessed=6_000_000, transcendentals=2_600_000),
        name="attention_backward",
    )(offsets, queries, grad_out, heads)


def reduce_kernel(part_ref, o_ref, chip_in, chip_sum, y_in, y_sum, pair_in, pair_sum, far_in, chip_sem, y_sem, pair_sem, far_sem, out_sem):
    y, z_hi, core, z_lo, x = place()
    kv = z_lo * 4 + x
    me = ctx_of(y, z_hi, core)
    mate = ctx_of(y, z_hi, 1 - core)
    pair = z_lo * 4 + x + 1 - 2 * (x % 2)
    odd = x % 2

    barrier = pltpu.get_barrier_semaphore()

    def greet(ctx, kv_idx):
        pl.semaphore_signal(barrier, inc=1, device_id=(ctx, kv_idx), device_id_type=MESH)

    greet(mate, kv)
    greet(ctx_of(y, 1 - z_hi, core), kv)
    for step in (1, 2, 3):
        greet(ctx_of((y + step) % 4, z_hi, core), kv)
    for step in range(1, 16):
        greet(me, (kv + step) % 16)
    pl.semaphore_wait(barrier, 20)

    def remote(src, dst, sems, ctx, kv_idx):
        copy = pltpu.make_async_remote_copy(src_ref=src, dst_ref=dst, send_sem=sems.at[0], recv_sem=sems.at[1],
                                            device_id=(ctx, kv_idx), device_id_type=MESH)
        copy.start()
        return copy

    sent = []
    order = (2, 1, 3, 0)
    chip = []
    for step in order:
        to_y = (y + step) % 4
        for half in range(2):
            chip.append(remote(part_ref.at[ctx_of(to_y, half, 1 - core)], chip_in.at[step, half],
                               chip_sem.at[step, half], mate, kv))
    along = []
    for nth, step in enumerate(order):
        to_y = (y + step) % 4
        for half in range(2):
            chip[2 * nth + half].wait_recv()
            both = part_ref[ctx_of(to_y, half, core)].astype(F32) + chip_in[step, half].astype(F32)
            chip_sum[step, half] = both.astype(BF16)
        if step:
            along.append(remote(chip_sum.at[step], y_in.at[step - 1], y_sem.at[step - 1],
                                ctx_of(to_y, z_hi, core), kv))
    for copy in along:
        copy.wait_recv()
    y_sum[...] = (chip_sum[0].astype(F32) + y_in[0].astype(F32) + y_in[1].astype(F32) + y_in[2].astype(F32)).astype(BF16)
    across = remote(y_sum.at[:, 1 - odd], pair_in, pair_sem, me, pair)
    across.wait_recv()
    pair_sum[...] = (y_sum[:, odd].astype(F32) + pair_in[...].astype(F32)).astype(BF16)
    other = remote(pair_sum.at[1 - z_hi], far_in, far_sem, ctx_of(y, 1 - z_hi, core), kv)
    other.wait_recv()
    o_ref[kv] = (pair_sum[z_hi].astype(F32) + far_in[...].astype(F32)).astype(BF16)
    spread = []
    for step in range(1, 16):
        spread.append(remote(o_ref.at[kv], o_ref.at[kv], out_sem.at[step - 1], me, (kv + step) % 16))
    for copy in chip + along + [across, other]:
        copy.wait_send()
    for copy in spread:
        copy.wait()


def reduce_grads(parts):
    vmem = pl.BlockSpec(memory_space=pltpu.VMEM)
    dma = pltpu.SemaphoreType.DMA
    return pl.pallas_call(
        reduce_kernel,
        out_shape=jax.ShapeDtypeStruct((2 * KVH, TOK, HD), BF16),
        in_specs=[vmem],
        out_specs=vmem,
        scratch_shapes=[
            pltpu.VMEM((4, 2, 2, TOK, HD), BF16), pltpu.VMEM((4, 2, 2, TOK, HD), BF16),
            pltpu.VMEM((3, 2, 2, TOK, HD), BF16), pltpu.VMEM((2, 2, TOK, HD), BF16),
            pltpu.VMEM((2, TOK, HD), BF16), pltpu.VMEM((2, TOK, HD), BF16), pltpu.VMEM((TOK, HD), BF16),
            dma((4, 2, 2)), dma((3, 2)), dma((2,)), dma((2,)), dma((15, 2)),
        ],
        compiler_params=pltpu.CompilerParams(collective_id=1, has_side_effects=True, vmem_limit_bytes=32 * 1024 * 1024),
        name="reduce_grads",
    )(parts)


def local(queries, key_heads, value_heads, grad_out, offsets):
    heads = gather_heads(key_heads, value_heads)
    grad_queries, parts = compute(offsets, queries, grad_out, heads)
    shares = reduce_grads(parts).reshape(KVH, 2, TOK, HD)
    wide = shares.transpose(1, 2, 0, 3).reshape(2, TOK, KVH * HD).astype(F32)
    return grad_queries, wide[0], wide[1]


def solution(mesh):
    in_specs = (P(None, "ctx", "kv"), P("ctx", None), P("ctx", None), P(None, "ctx", "kv"), P())
    out_specs = (P(None, "ctx", "kv"), P("ctx", None), P("ctx", None))
    return jax.shard_map(local, mesh=mesh, in_specs=in_specs, out_specs=out_specs, check_vma=False)
```

```python
import jax
import jax.numpy as jnp
from jax import lax
from jax.experimental import pallas as pl
from jax.experimental.pallas import tpu as pltpu
from jax.sharding import PartitionSpec as P

KVH = 8
HD = 128
TOK = 192
HALF = 96
CTX = 16
TOTAL = CTX * TOK
BLOCKS = 2 * CTX
LAYERS = 2
HEADS = 4
UNITS = LAYERS * HEADS
ROWS = UNITS * HALF
TILE = 384
TILE_BLOCKS = TILE // HALF
TILES = TOTAL // TILE
SLOTS = TILES + 1
SPLIT = 2
CHUNK = HALF // SPLIT
CHUNKS = 2 * SPLIT
SCALE = HD ** -0.5
EXP2_SCALE = SCALE * 1.4426950408889634
MESH = pl.DeviceIdType.MESH
BF16 = jnp.bfloat16
F32 = jnp.float32
KEYS, VALUES = 0, 1
RANK_OF, BLOCK_AT, TILE_OF = 0, 1, 2


def ctx_of(y, z_hi, core):
    return y * 4 + z_hi * 2 + core


def head_of(z_lo, x):
    return z_lo * 2 + x // 2


def kernel(place_ref, q_ref, g_ref, k_ref, v_ref, dq_ref, gk_ref, gv_ref,
           all_k, all_v, sorted_k, sorted_v, qs, gs, s_scr, p_scr, d_scr, k_acc, v_acc, q_acc, top_hist, sum_hist, delta_hist, stats, dq_out,
           parts, chip_in, chip_sum, y_in, y_sum, far_in, shares, grads,
           in_sem, own_sem, cross_sem, near_sem, over_sem, mate_sem, chip_sem, y_sem, far_sem, z_sem, x_sem, out_sem):
    ctx, kv = lax.axis_index("ctx"), lax.axis_index("kv")
    y, z_hi, core, z_lo, x = ctx // 4, (ctx // 2) % 2, ctx % 2, kv // 4, kv % 4
    mate = ctx_of(y, z_hi, 1 - core)
    far = ctx_of(y, 1 - z_hi, core)
    odd = x % 2
    pair = z_lo * 4 + x + 1 - 2 * odd
    y_peers = [ctx_of((y + step) % 4, z_hi, core) for step in (1, 2, 3)]
    x_peers = [z_lo * 4 + (x + step) % 4 for step in (1, 2, 3)]
    z_peers = [(z_lo + step) % 4 * 4 + x for step in (1, 2, 3)]
    at_low, at_high = z_lo == 0, z_lo == 3
    at_edge = jnp.logical_or(at_low, at_high)
    nt_dims = (((1,), (1,)), ((), ()))
    tn_dims = (((0,), (0,)), ((), ()))

    for nth, (ref, dst) in enumerate(((q_ref, qs), (g_ref, gs))):
        for half in range(2):
            for unit in range(UNITS):
                layer, head = divmod(unit, HEADS)
                pltpu.make_async_copy(
                    ref.at[layer, half * HALF:(half + 1) * HALF, head * HD:(head + 1) * HD],
                    dst.at[half, unit * HALF:(unit + 1) * HALF], in_sem.at[nth]).start()

    barrier = pltpu.get_barrier_semaphore()
    peers = [(mate, kv), (far, kv), (far, pair)] + [(c, kv) for c in y_peers] + [(ctx, k) for k in x_peers + z_peers]
    peers.append((far, jnp.where(z_lo < 2, 3, 0) * 4 + x))
    for peer in peers:
        pl.semaphore_signal(barrier, inc=1, device_id=peer, device_id_type=MESH)
    pl.semaphore_wait(barrier, jnp.where(at_edge, 14, 12))

    def describe(src, dst, send_sem, recv_sem, ctx_idx, kv_idx):
        return pltpu.make_async_remote_copy(src_ref=src, dst_ref=dst, send_sem=send_sem, recv_sem=recv_sem,
                                            device_id=(ctx_idx, kv_idx), device_id_type=MESH)

    def remote(src, dst, sems, ctx_idx, kv_idx):
        copy = describe(src, dst, sems.at[0], sems.at[1], ctx_idx, kv_idx)
        copy.start()
        return copy

    def head_slice(part, head):
        return (k_ref, v_ref)[part].at[:, :, pl.ds(pl.multiple_of(head * HD, HD), HD)]

    def tokens_of(part, ctx_idx):
        return (all_k, all_v)[part].at[pl.ds(2 * ctx_idx, 2)]

    def cross(part, act):
        for edge, targets in ((at_low, (2, 3)), (at_high, (1, 0))):
            @pl.when(edge)
            def _():
                for nth, target in enumerate(targets):
                    act(describe(head_slice(part, head_of(target, x)), tokens_of(part, ctx),
                                 cross_sem.at[part, 1 + nth], cross_sem.at[part, 0], far, target * 4 + x))

    head = head_of(z_lo, x)
    near, over, to_mate = {}, {}, {}

    def send_near(part):
        near[part] = [remote(head_slice(part, head), tokens_of(part, ctx), near_sem.at[part, step - 1], y_peers[step - 1], kv)
                      for step in (1, 2, 3)]

    def send_over(part):
        pltpu.make_async_copy(tokens_of(part, far), tokens_of(part, far), cross_sem.at[part, 0]).wait()
        over[part] = [remote(tokens_of(part, far), tokens_of(part, far), over_sem.at[part, step - 1], y_peers[step - 1], kv)
                      for step in (1, 2, 3)]

    def send_mate(part, step, half):
        idx = ctx_of((y - step + 4) % 4, half, core)
        to_mate.setdefault(part, []).append(
            remote(tokens_of(part, idx), tokens_of(part, idx), mate_sem.at[part, len(to_mate.get(part, []))], mate, kv))

    own = [pltpu.make_async_copy(head_slice(part, head), tokens_of(part, ctx), own_sem.at[part]) for part in (KEYS, VALUES)]
    cross(KEYS, lambda copy: copy.start())
    send_near(KEYS)
    for copy in own:
        copy.start()
    cross(KEYS, lambda copy: copy.wait_send())
    cross(VALUES, lambda copy: copy.start())
    own[KEYS].wait()
    send_mate(KEYS, 0, z_hi)
    send_over(KEYS)
    send_mate(KEYS, 0, 1 - z_hi)
    for step in (1, 3, 2):
        near[KEYS][step - 1].wait_recv()
        send_mate(KEYS, step, z_hi)
    send_near(VALUES)
    own[VALUES].wait()
    send_mate(VALUES, 0, z_hi)
    for step in (1, 3, 2):
        over[KEYS][step - 1].wait_recv()
        send_mate(KEYS, step, 1 - z_hi)
    send_over(VALUES)
    send_mate(VALUES, 0, 1 - z_hi)
    for copy in to_mate[KEYS]:
        copy.wait_recv()

    def sort(part):
        for rank in range(BLOCKS):
            first = rank % TILE_BLOCKS * HALF
            (sorted_k, sorted_v)[part][rank // TILE_BLOCKS, first:first + HALF] = (all_k, all_v)[part][place_ref[BLOCK_AT, rank]]

    sort(KEYS)
    pltpu.make_async_copy(qs, qs, in_sem.at[0]).wait()
    pltpu.make_async_copy(gs, gs, in_sem.at[1]).wait()

    start_0, start_1 = place_ref[RANK_OF, 2 * ctx] * HALF, place_ref[RANK_OF, 2 * ctx + 1] * HALF
    count_0 = place_ref[TILE_OF, 2 * ctx] + 1
    count_1 = SLOTS - count_0

    def slot_of(slot):
        half = (slot >= count_0).astype(jnp.int32)
        tile = slot - count_0 * half
        return half, tile, tile, pl.ds(pl.multiple_of(slot * TILE, TILE), TILE)

    def carried(slot):
        return (slot != count_0).astype(F32)

    def fold(tile, op):
        return op(tile.reshape(TILE // 8, 8, ROWS), axis=0)

    def score_step(slot, top):
        half, tile, keys, rows = slot_of(slot)
        s = lax.dot_general(sorted_k[keys], qs[half], nt_dims, preferred_element_type=F32)
        ahead = lax.broadcasted_iota(jnp.int32, (TILE, ROWS), 0) - lax.broadcasted_iota(jnp.int32, (TILE, ROWS), 1) % HALF
        s = jnp.where(ahead <= start_0 + (start_1 - start_0) * half - tile * TILE, s, -1e30)
        s_scr[rows] = s
        keep = carried(slot)
        top = jnp.maximum(top * keep - 1e30 * (1.0 - keep), fold(s, jnp.max))
        top_hist[slot] = top
        return top

    top = lax.fori_loop(0, 4, score_step, jnp.full((8, ROWS), -1e30, F32))
    for step in (1, 3, 2):
        near[VALUES][step - 1].wait_recv()
        send_mate(VALUES, step, z_hi)
    for step in (1, 3, 2):
        over[VALUES][step - 1].wait_recv()
        send_mate(VALUES, step, 1 - z_hi)
    lax.fori_loop(4, SLOTS, score_step, top)
    for half, last in enumerate((count_0 - 1, SLOTS - 1)):
        stats[half, 0] = jnp.broadcast_to(jnp.max(top_hist[last], axis=0, keepdims=True), (8, ROWS))
    for copy in to_mate[VALUES]:
        copy.wait_recv()
    sort(VALUES)

    def sum_step(slot, sums):
        half, tile, keys, rows = slot_of(slot)
        weight = jnp.exp2((s_scr[rows] - stats[half, 0][:1]) * EXP2_SCALE)
        grad_prob = lax.dot_general(sorted_v[keys], gs[half], nt_dims, preferred_element_type=F32)
        s_scr[rows] = weight
        p_scr[rows] = grad_prob
        keep = carried(slot)
        total, delta = sums[0] * keep + fold(weight, jnp.sum), sums[1] * keep + fold(weight * grad_prob, jnp.sum)
        sum_hist[slot], delta_hist[slot] = total, delta
        return total, delta

    zero = jnp.zeros((8, ROWS), F32)
    lax.fori_loop(0, SLOTS, sum_step, (zero, zero))
    for half, last in enumerate((count_0 - 1, SLOTS - 1)):
        inv = 1.0 / jnp.sum(sum_hist[last], axis=0, keepdims=True)
        delta = jnp.sum(delta_hist[last], axis=0, keepdims=True) * inv
        stats[half, 1] = jnp.broadcast_to(inv, (8, ROWS))
        stats[half, 2] = jnp.broadcast_to(delta, (8, ROWS))

    def value_step(slot, _):
        half, tile, keys, rows = slot_of(slot)
        prob = s_scr[rows] * stats[half, 1][:1]
        v_acc[pl.ds(slot * TILE_BLOCKS, TILE_BLOCKS)] = jnp.dot(prob.astype(BF16), gs[half], preferred_element_type=F32).reshape(TILE_BLOCKS, HALF, HD)
        d_scr[rows] = (prob * (p_scr[rows] - stats[half, 2][:1])).astype(BF16)
        return 0

    def key_step(slot, _):
        half, tile, keys, rows = slot_of(slot)
        k_acc[pl.ds(slot * TILE_BLOCKS, TILE_BLOCKS)] = jnp.dot(d_scr[rows], qs[half], preferred_element_type=F32).reshape(TILE_BLOCKS, HALF, HD)
        return 0

    def query_step(slot, _):
        half, tile, keys, rows = slot_of(slot)
        term = lax.dot_general(d_scr[rows], sorted_k[keys], tn_dims, preferred_element_type=F32)
        q_acc[slot] = term + q_acc[jnp.maximum(slot - 1, 0)] * carried(slot)
        return 0

    def by_tokens(part, acc, scale):
        for block in range(BLOCKS):
            rank = place_ref[RANK_OF, block]
            in_0 = (rank < count_0 * TILE_BLOCKS).astype(jnp.int32)
            in_1 = (rank < count_1 * TILE_BLOCKS).astype(jnp.int32)
            both = (acc[rank * in_0] * (in_0.astype(F32) * scale)
                    + acc[(count_0 * TILE_BLOCKS + rank) * in_1] * (in_1.astype(F32) * scale))
            parts[part, block // 2 % 2, block // 8, block // 4 % 2, block % 2] = both.astype(BF16)

    chunks = {VALUES: range(SPLIT), KEYS: range(SPLIT, CHUNKS)}
    chip, along, across, along_z, along_x = {}, {}, {}, {}, {}

    def rows_of(chunk):
        return slice(chunk % SPLIT * CHUNK, (chunk % SPLIT + 1) * CHUNK)

    def send_chip(part):
        for chunk in chunks[part]:
            chip[chunk] = remote(parts.at[part, 1 - core, :, :, :, rows_of(chunk)], chip_in.at[chunk], chip_sem.at[chunk], mate, kv)

    def send_y(part):
        for chunk in chunks[part]:
            chip[chunk].wait_recv()
            along[chunk] = []
            for step in (2, 1, 3, 0):
                to_y = (y + step) % 4
                both = parts[part, core, to_y, :, :, rows_of(chunk)].astype(F32) + chip_in[chunk, to_y].astype(F32)
                chip_sum[chunk, step] = both.astype(BF16)
                if step:
                    along[chunk].append(remote(chip_sum.at[chunk, step], y_in.at[chunk, step - 1],
                                               y_sem.at[chunk, step - 1], y_peers[step - 1], kv))

    def send_far(part):
        for chunk in chunks[part]:
            for copy in along[chunk]:
                copy.wait_recv()
            total = chip_sum[chunk, 0].astype(F32)
            for step in range(3):
                total += y_in[chunk, step].astype(F32)
            y_sum[chunk] = total.astype(BF16)
            across[chunk] = [
                remote(y_sum.at[chunk, 1 - z_hi, 1 - odd], far_in.at[chunk, 0], far_sem.at[chunk, 0], far, pair),
                remote(y_sum.at[chunk, 1 - z_hi, odd], far_in.at[chunk, 1], far_sem.at[chunk, 1], far, kv),
                remote(y_sum.at[chunk, z_hi, 1 - odd], far_in.at[chunk, 2], far_sem.at[chunk, 2], ctx, pair)]

    def send_x(chunk, z_step):
        slot = shares.at[chunk, x, (z_lo - z_step + 4) % 4]
        along_x.setdefault(chunk, []).extend(
            remote(slot, slot, x_sem.at[chunk, z_step, step - 1], ctx, x_peers[step - 1]) for step in (2, 1, 3))

    def send_z(part):
        for chunk in chunks[part]:
            for copy in across[chunk]:
                copy.wait_recv()
            total = y_sum[chunk, z_hi, odd].astype(F32)
            for nth in range(3):
                total += far_in[chunk, nth].astype(F32)
            shares[chunk, x, z_lo] = total.astype(BF16)
            slot = shares.at[chunk, x, z_lo]
            along_z[chunk] = [remote(slot, slot, z_sem.at[chunk, step - 1], ctx, z_peers[step - 1]) for step in (1, 2, 3)]
            send_x(chunk, 0)

    def pass_on(part):
        for chunk in chunks[part]:
            for z_step in (1, 2, 3):
                along_z[chunk][z_step - 1].wait_recv()
                send_x(chunk, z_step)

    def finish(part):
        for chunk in chunks[part]:
            for copy in along_x[chunk]:
                copy.wait_recv()
            rows = rows_of(chunk)
            for z_idx in range(4):
                for x_idx in range(4):
                    first = (x_idx % 2) * HALF
                    col = head_of(z_idx, x_idx) * HD
                    grads[part, first + rows.start:first + rows.stop, col:col + HD] = shares[chunk, x_idx, z_idx].astype(F32)
        copy = pltpu.make_async_copy(grads.at[part], (gk_ref, gv_ref)[part], out_sem.at[part])
        copy.start()
        return copy

    lax.fori_loop(0, SLOTS, value_step, 0)
    by_tokens(VALUES, v_acc, 1.0)
    send_chip(VALUES)
    lax.fori_loop(0, SLOTS, key_step, 0)
    send_y(VALUES)
    by_tokens(KEYS, k_acc, SCALE)
    send_chip(KEYS)
    q_acc[0] = jnp.zeros((ROWS, HD), F32)
    lax.fori_loop(0, 4, query_step, 0)
    send_y(KEYS)
    lax.fori_loop(4, SLOTS, query_step, 0)
    send_far(VALUES)
    for half in range(2):
        last = count_0 - 1 if half == 0 else SLOTS - 1
        for unit in range(UNITS):
            layer, head_idx = divmod(unit, HEADS)
            dq_out[layer, half * HALF:(half + 1) * HALF, head_idx * HD:(head_idx + 1) * HD] = (
                q_acc[last, unit * HALF:(unit + 1) * HALF] * SCALE).astype(BF16)
    dq_copy = pltpu.make_async_copy(dq_out, dq_ref, out_sem.at[2])
    dq_copy.start()
    send_far(KEYS)
    send_z(VALUES)
    send_z(KEYS)
    pass_on(VALUES)
    pass_on(KEYS)
    written = [dq_copy, finish(VALUES), finish(KEYS)]
    for copy in written:
        copy.wait()
    cross(VALUES, lambda copy: copy.wait_send())
    for group in (near, over, to_mate, along, across, along_z, along_x):
        for copies in group.values():
            for copy in copies:
                copy.wait_send()
    for copy in chip.values():
        copy.wait_send()


def local(queries, key_heads, value_heads, grad_out, offsets):
    ranks = jnp.arange(BLOCKS, dtype=jnp.int32)
    blocks = jnp.sum(jnp.where(offsets[None, :] == ranks[:, None] * HALF, ranks[None, :], 0), axis=1)
    places = jnp.stack([offsets // HALF, blocks, offsets // TILE])
    dma, vmem = pltpu.SemaphoreType.DMA, pltpu.VMEM
    hbm = pl.BlockSpec(memory_space=pl.ANY)
    smem = pl.BlockSpec(memory_space=pltpu.SMEM)
    grads = jax.ShapeDtypeStruct((TOK, KVH * HD), F32)
    return pl.pallas_call(
        kernel,
        out_shape=(jax.ShapeDtypeStruct(queries.shape, BF16), grads, grads),
        in_specs=[smem, hbm, hbm, hbm, hbm],
        out_specs=(hbm, hbm, hbm),
        scratch_shapes=[
            vmem((BLOCKS, HALF, HD), BF16), vmem((BLOCKS, HALF, HD), BF16), vmem((TILES, TILE, HD), BF16), vmem((TILES, TILE, HD), BF16),
            vmem((2, ROWS, HD), BF16), vmem((2, ROWS, HD), BF16),
            vmem((SLOTS * TILE, ROWS), F32), vmem((SLOTS * TILE, ROWS), F32), vmem((SLOTS * TILE, ROWS), BF16),
            vmem((SLOTS * TILE_BLOCKS, HALF, HD), F32), vmem((SLOTS * TILE_BLOCKS, HALF, HD), F32), vmem((SLOTS, ROWS, HD), F32),
            vmem((SLOTS, 8, ROWS), F32), vmem((SLOTS, 8, ROWS), F32), vmem((SLOTS, 8, ROWS), F32), vmem((2, 3, 8, ROWS), F32),
            vmem((LAYERS, TOK, HEADS * HD), BF16),
            vmem((2, 2, 4, 2, 2, HALF, HD), BF16),
            vmem((CHUNKS, 4, 2, 2, CHUNK, HD), BF16), vmem((CHUNKS, 4, 2, 2, CHUNK, HD), BF16),
            vmem((CHUNKS, 3, 2, 2, CHUNK, HD), BF16), vmem((CHUNKS, 2, 2, CHUNK, HD), BF16),
            vmem((CHUNKS, 3, CHUNK, HD), BF16), vmem((CHUNKS, 4, 4, CHUNK, HD), BF16),
            vmem((2, TOK, KVH * HD), F32),
            dma((2,)), dma((2,)), dma((2, 3)), dma((2, 3, 2)), dma((2, 3, 2)), dma((2, 8, 2)),
            dma((CHUNKS, 2)), dma((CHUNKS, 3, 2)), dma((CHUNKS, 3, 2)), dma((CHUNKS, 3, 2)), dma((CHUNKS, 4, 3, 2)), dma((3,)),
        ],
        compiler_params=pltpu.CompilerParams(collective_id=0, has_side_effects=True, vmem_limit_bytes=58 * 1024 * 1024),
        cost_estimate=pl.CostEstimate(flops=3_400_000_000, bytes_accessed=6_000_000, transcendentals=2_600_000),
        name="attention_backward",
    )(places, queries, grad_out, key_heads.reshape(2, HALF, KVH * HD), value_heads.reshape(2, HALF, KVH * HD))


def solution(mesh):
    in_specs = (P(None, "ctx", "kv"), P("ctx", None), P("ctx", None), P(None, "ctx", "kv"), P())
    out_specs = (P(None, "ctx", "kv"), P("ctx", None), P("ctx", None))
    return jax.shard_map(local, mesh=mesh, in_specs=in_specs, out_specs=out_specs, check_vma=False)
```

```python
import jax
import jax.numpy as jnp
from jax import lax
from jax.experimental import pallas as pl
from jax.experimental.pallas import tpu as pltpu
from jax.sharding import PartitionSpec as P

KVH = 8
HD = 128
TOK = 192
HALF = 96
CTX = 16
TOTAL = CTX * TOK
BLOCKS = 2 * CTX
LAYERS = 2
HEADS = 4
UNITS = LAYERS * HEADS
ROWS = UNITS * HALF
TILE = 384
TILE_BLOCKS = TILE // HALF
TILES = TOTAL // TILE
SLOTS = TILES + 1
SPLIT = 2
CHUNK = HALF // SPLIT
CHUNKS = 2 * SPLIT
SCALE = HD ** -0.5
EXP2_SCALE = SCALE * 1.4426950408889634
MESH = pl.DeviceIdType.MESH
BF16 = jnp.bfloat16
F32 = jnp.float32
UNROLL = 3
KEYS, VALUES = 0, 1
RANK_OF, BLOCK_AT, TILE_OF = 0, 1, 2


def ctx_of(y, z_hi, core):
    return y * 4 + z_hi * 2 + core


def head_of(z_lo, x):
    return z_lo * 2 + x // 2


def kernel(place_ref, q_ref, g_ref, k_ref, v_ref, dq_ref, out_ref,
           all_k, all_v, sorted_k, sorted_v, qs, gs, s_scr, p_scr, d_scr, k_acc, v_acc, q_acc, top_hist, sum_hist, delta_hist, stats, dq_out,
           parts, chip_in, chip_sum, y_in, y_sum, z_in, shares,
           in_sem, own_sem, cross_sem, near_sem, over_sem, mate_sem, chip_sem, y_sem, z_sem, x_sem, out_sem):
    ctx, kv = lax.axis_index("ctx"), lax.axis_index("kv")
    y, z_hi, core, z_lo, x = ctx // 4, (ctx // 2) % 2, ctx % 2, kv // 4, kv % 4
    mate = ctx_of(y, z_hi, 1 - core)
    far = ctx_of(y, 1 - z_hi, core)
    odd = x % 2
    pair = z_lo * 4 + x + 1 - 2 * odd
    y_peers = [ctx_of((y + step) % 4, z_hi, core) for step in (1, 2, 3)]
    x_peers = [z_lo * 4 + (x + step) % 4 for step in (1, 2, 3)]
    z_peers = [(z_lo + step) % 4 * 4 + x for step in (1, 2, 3)]
    at_low, at_high = z_lo == 0, z_lo == 3
    nt_dims = (((1,), (1,)), ((), ()))
    tn_dims = (((0,), (0,)), ((), ()))

    for nth, (ref, dst) in enumerate(((q_ref, qs), (g_ref, gs))):
        for half in range(2):
            for unit in range(UNITS):
                layer, head = divmod(unit, HEADS)
                pltpu.make_async_copy(
                    ref.at[layer, half * HALF:(half + 1) * HALF, head * HD:(head + 1) * HD],
                    dst.at[half, unit * HALF:(unit + 1) * HALF], in_sem.at[nth]).start()

    barrier = pltpu.get_barrier_semaphore()
    peers = [(mate, kv)] + [(c, k) for c in y_peers for k in (kv, pair)] + [(ctx, k) for k in x_peers + z_peers]
    peers += [(far, z_idx * 4 + x) for z_idx in range(4)]
    for peer in peers:
        pl.semaphore_signal(barrier, inc=1, device_id=peer, device_id_type=MESH)
    pl.semaphore_wait(barrier, len(peers))

    def describe(src, dst, send_sem, recv_sem, ctx_idx, kv_idx):
        return pltpu.make_async_remote_copy(src_ref=src, dst_ref=dst, send_sem=send_sem, recv_sem=recv_sem,
                                            device_id=(ctx_idx, kv_idx), device_id_type=MESH)

    def remote(src, dst, sems, ctx_idx, kv_idx):
        copy = describe(src, dst, sems.at[0], sems.at[1], ctx_idx, kv_idx)
        copy.start()
        return copy

    def head_slice(part, head):
        return (k_ref, v_ref)[part].at[:, :, pl.ds(pl.multiple_of(head * HD, HD), HD)]

    def tokens_of(part, ctx_idx):
        return (all_k, all_v)[part].at[pl.ds(2 * ctx_idx, 2)]

    def cross(part, act):
        for edge, targets in ((at_low, (2, 3)), (at_high, (1, 0))):
            @pl.when(edge)
            def _():
                for nth, target in enumerate(targets):
                    act(describe(head_slice(part, head_of(target, x)), tokens_of(part, ctx),
                                 cross_sem.at[part, 1 + nth], cross_sem.at[part, 0], far, target * 4 + x))

    head = head_of(z_lo, x)
    near, over, to_mate = {}, {}, {}

    def send_near(part):
        near[part] = [remote(head_slice(part, head), tokens_of(part, ctx), near_sem.at[part, step - 1], y_peers[step - 1], kv)
                      for step in (1, 2, 3)]

    def send_over(part):
        pltpu.make_async_copy(tokens_of(part, far), tokens_of(part, far), cross_sem.at[part, 0]).wait()
        over[part] = [remote(tokens_of(part, far), tokens_of(part, far), over_sem.at[part, step - 1], y_peers[step - 1], kv)
                      for step in (1, 2, 3)]

    def send_mate(part, step, half):
        idx = ctx_of((y - step + 4) % 4, half, core)
        to_mate.setdefault(part, []).append(
            remote(tokens_of(part, idx), tokens_of(part, idx), mate_sem.at[part, len(to_mate.get(part, []))], mate, kv))

    own = [pltpu.make_async_copy(head_slice(part, head), tokens_of(part, ctx), own_sem.at[part]) for part in (KEYS, VALUES)]
    cross(KEYS, lambda copy: copy.start())
    send_near(KEYS)
    for copy in own:
        copy.start()
    cross(KEYS, lambda copy: copy.wait_send())
    cross(VALUES, lambda copy: copy.start())
    own[KEYS].wait()
    send_mate(KEYS, 0, z_hi)
    for copy in near[KEYS]:
        copy.wait_send()
    send_near(VALUES)
    own[VALUES].wait()
    send_mate(VALUES, 0, z_hi)
    send_over(KEYS)
    send_mate(KEYS, 0, 1 - z_hi)
    for step in (1, 3, 2):
        near[KEYS][step - 1].wait_recv()
        send_mate(KEYS, step, z_hi)
    send_over(VALUES)
    send_mate(VALUES, 0, 1 - z_hi)
    for step in (1, 3, 2):
        over[KEYS][step - 1].wait_recv()
        send_mate(KEYS, step, 1 - z_hi)
    for step in (1, 3, 2):
        near[VALUES][step - 1].wait_recv()
        send_mate(VALUES, step, z_hi)
    for copy in to_mate[KEYS]:
        copy.wait_recv()

    def sort(part):
        for rank in range(BLOCKS):
            first = rank % TILE_BLOCKS * HALF
            (sorted_k, sorted_v)[part][rank // TILE_BLOCKS, first:first + HALF] = (all_k, all_v)[part][place_ref[BLOCK_AT, rank]]

    sort(KEYS)
    pltpu.make_async_copy(qs, qs, in_sem.at[0]).wait()
    pltpu.make_async_copy(gs, gs, in_sem.at[1]).wait()

    start_0, start_1 = place_ref[RANK_OF, 2 * ctx] * HALF, place_ref[RANK_OF, 2 * ctx + 1] * HALF
    count_0 = place_ref[TILE_OF, 2 * ctx] + 1
    count_1 = SLOTS - count_0

    def slot_of(slot):
        half = (slot >= count_0).astype(jnp.int32)
        tile = slot - count_0 * half
        return half, tile, tile, pl.ds(pl.multiple_of(slot * TILE, TILE), TILE)

    def carried(slot):
        return (slot != count_0).astype(F32)

    def fold(tile, op):
        return op(tile.reshape(TILE // 8, 8, ROWS), axis=0)

    def score_step(slot, top):
        half, tile, keys, rows = slot_of(slot)
        s = lax.dot_general(sorted_k[keys], qs[half], nt_dims, preferred_element_type=F32)
        ahead = lax.broadcasted_iota(jnp.int32, (TILE, ROWS), 0) - lax.broadcasted_iota(jnp.int32, (TILE, ROWS), 1) % HALF
        s = jnp.where(ahead <= start_0 + (start_1 - start_0) * half - tile * TILE, s, -1e30)
        s_scr[rows] = s
        keep = carried(slot)
        top = jnp.maximum(top * keep - 1e30 * (1.0 - keep), fold(s, jnp.max))
        top_hist[slot] = top
        return top

    top = lax.fori_loop(0, SLOTS - UNROLL, score_step, jnp.full((8, ROWS), -1e30, F32), unroll=UNROLL)
    for step in (1, 3, 2):
        over[VALUES][step - 1].wait_recv()
        send_mate(VALUES, step, 1 - z_hi)
    lax.fori_loop(SLOTS - UNROLL, SLOTS, score_step, top, unroll=UNROLL)
    for half, last in enumerate((count_0 - 1, SLOTS - 1)):
        stats[half, 0] = jnp.broadcast_to(jnp.max(top_hist[last], axis=0, keepdims=True), (8, ROWS))
    for copy in to_mate[VALUES]:
        copy.wait_recv()
    sort(VALUES)

    def sum_step(slot, sums):
        half, tile, keys, rows = slot_of(slot)
        weight = jnp.exp2((s_scr[rows] - stats[half, 0][:1]) * EXP2_SCALE)
        grad_prob = lax.dot_general(sorted_v[keys], gs[half], nt_dims, preferred_element_type=F32)
        s_scr[rows] = weight
        p_scr[rows] = grad_prob
        keep = carried(slot)
        total, delta = sums[0] * keep + fold(weight, jnp.sum), sums[1] * keep + fold(weight * grad_prob, jnp.sum)
        sum_hist[slot], delta_hist[slot] = total, delta
        return total, delta

    zero = jnp.zeros((8, ROWS), F32)
    lax.fori_loop(0, SLOTS, sum_step, (zero, zero), unroll=UNROLL)
    for half, last in enumerate((count_0 - 1, SLOTS - 1)):
        inv = 1.0 / jnp.sum(sum_hist[last], axis=0, keepdims=True)
        delta = jnp.sum(delta_hist[last], axis=0, keepdims=True) * inv
        stats[half, 1] = jnp.broadcast_to(inv, (8, ROWS))
        stats[half, 2] = jnp.broadcast_to(delta, (8, ROWS))

    def value_step(slot, _):
        half, tile, keys, rows = slot_of(slot)
        prob = s_scr[rows] * stats[half, 1][:1]
        v_acc[pl.ds(slot * TILE_BLOCKS, TILE_BLOCKS)] = jnp.dot(prob.astype(BF16), gs[half], preferred_element_type=F32).reshape(TILE_BLOCKS, HALF, HD)
        d_scr[rows] = (prob * (p_scr[rows] - stats[half, 2][:1])).astype(BF16)
        return 0

    def key_step(slot, _):
        half, tile, keys, rows = slot_of(slot)
        k_acc[pl.ds(slot * TILE_BLOCKS, TILE_BLOCKS)] = jnp.dot(d_scr[rows], qs[half], preferred_element_type=F32).reshape(TILE_BLOCKS, HALF, HD)
        return 0

    def query_step(slot, _):
        half, tile, keys, rows = slot_of(slot)
        term = lax.dot_general(d_scr[rows], sorted_k[keys], tn_dims, preferred_element_type=F32)
        q_acc[slot] = term + q_acc[jnp.maximum(slot - 1, 0)] * carried(slot)
        return 0

    def by_tokens(part, acc, scale):
        for block in range(BLOCKS):
            rank = place_ref[RANK_OF, block]
            in_0 = (rank < count_0 * TILE_BLOCKS).astype(jnp.int32)
            in_1 = (rank < count_1 * TILE_BLOCKS).astype(jnp.int32)
            both = (acc[rank * in_0] * (in_0.astype(F32) * scale)
                    + acc[(count_0 * TILE_BLOCKS + rank) * in_1] * (in_1.astype(F32) * scale))
            parts[part, block // 2 % 2, block // 8, block % 2, block // 4 % 2] = both.astype(BF16)

    chunks = {KEYS: range(SPLIT), VALUES: range(SPLIT, CHUNKS)}
    chip, along, along_z, along_x = {}, {}, {}, {}

    def rows_of(chunk):
        return slice(chunk % SPLIT * CHUNK, (chunk % SPLIT + 1) * CHUNK)

    def send_chip(part):
        for chunk in chunks[part]:
            chip[chunk] = remote(parts.at[part, 1 - core, :, :, :, rows_of(chunk)], chip_in.at[chunk], chip_sem.at[chunk], mate, kv)

    def send_y(part):
        for chunk in chunks[part]:
            chip[chunk].wait_recv()
            along[chunk] = []
            for step in (2, 1, 3, 0):
                to_y = (y + step) % 4
                both = parts[part, core, to_y, :, :, rows_of(chunk)].astype(F32) + chip_in[chunk, to_y].astype(F32)
                chip_sum[chunk, step] = both.astype(BF16)
                to_ctx = y_peers[step - 1] if step else ctx
                for other in ((1, 0) if step else (1,)):
                    nth = 2 * step + other - 1
                    along[chunk].append(remote(chip_sum.at[chunk, step, 1 - odd if other else odd], y_in.at[chunk, nth],
                                               y_sem.at[chunk, nth], to_ctx, pair if other else kv))

    def send_z(part):
        for chunk in chunks[part]:
            for copy in along[chunk]:
                copy.wait_recv()
            total = chip_sum[chunk, 0, odd].astype(F32)
            for nth in range(7):
                total += y_in[chunk, nth].astype(F32)
            y_sum[chunk] = total.astype(BF16)
            along_z[chunk] = [
                remote(y_sum.at[chunk, 1 - z_hi], z_in.at[chunk, 1, z_lo], z_sem.at[chunk, 1, step], far, (z_lo + step) % 4 * 4 + x)
                for step in (0, 3, 1, 2)]
            along_z[chunk] += [
                remote(y_sum.at[chunk, z_hi], z_in.at[chunk, 0, z_lo], z_sem.at[chunk, 0, step], ctx, z_peers[step - 1])
                for step in (3, 2, 1)]
            z_in[chunk, 0, z_lo] = y_sum[chunk, z_hi]

    def send_x(part):
        for chunk in chunks[part]:
            for copy in along_z[chunk]:
                copy.wait_recv()
            shares[chunk, x] = (z_in[chunk, 0].astype(F32) + z_in[chunk, 1].astype(F32)).astype(BF16)
            slot = shares.at[chunk, x]
            along_x[chunk] = [remote(slot, slot, x_sem.at[chunk, step - 1], ctx, x_peers[step - 1]) for step in (2, 1, 3)]

    written = []

    def finish(part):
        for chunk in chunks[part]:
            for copy in along_x[chunk]:
                copy.wait_recv()
            written.append(pltpu.make_async_copy(shares.at[chunk], out_ref.at[chunk], out_sem.at[1 + chunk]))
            written[-1].start()

    lax.fori_loop(0, SLOTS, value_step, 0, unroll=UNROLL)
    by_tokens(VALUES, v_acc, 1.0)
    send_chip(VALUES)
    lax.fori_loop(0, SLOTS, key_step, 0, unroll=UNROLL)
    send_y(VALUES)
    by_tokens(KEYS, k_acc, SCALE)
    send_chip(KEYS)
    q_acc[0] = jnp.zeros((ROWS, HD), F32)
    lax.fori_loop(0, 4, query_step, 0)
    send_y(KEYS)
    lax.fori_loop(4, SLOTS, query_step, 0)
    send_z(VALUES)
    for half in range(2):
        last = count_0 - 1 if half == 0 else SLOTS - 1
        for unit in range(UNITS):
            layer, head_idx = divmod(unit, HEADS)
            dq_out[layer, half * HALF:(half + 1) * HALF, head_idx * HD:(head_idx + 1) * HD] = (
                q_acc[last, unit * HALF:(unit + 1) * HALF] * SCALE).astype(BF16)
    written.append(pltpu.make_async_copy(dq_out, dq_ref, out_sem.at[0]))
    written[-1].start()
    send_z(KEYS)
    send_x(VALUES)
    send_x(KEYS)
    finish(VALUES)
    finish(KEYS)
    for copy in written:
        copy.wait()
    cross(VALUES, lambda copy: copy.wait_send())
    for copy in near[VALUES]:
        copy.wait_send()
    for group in (over, to_mate, along, along_z, along_x):
        for copies in group.values():
            for copy in copies:
                copy.wait_send()
    for copy in chip.values():
        copy.wait_send()


def place_kernel(off_ref, place_ref):
    for block in range(BLOCKS):
        rank = lax.div(off_ref[block], HALF)
        place_ref[RANK_OF, block] = rank
        place_ref[BLOCK_AT, rank] = block
        place_ref[TILE_OF, block] = lax.div(rank, TILE_BLOCKS)


def write_kernel(dq_in, share_ref, dq_ref, gk_ref, gv_ref):
    dq_ref[...] = dq_in[...]
    for part, ref in enumerate((gk_ref, gv_ref)):
        for pair in range(2):
            for z_lo in range(4):
                col = head_of(z_lo, 2 * pair) * HD
                ref[:, col:col + HD] = share_ref[part, 0, pair, 0, z_lo].astype(F32)


def local(queries, key_heads, value_heads, grad_out, offsets):
    dma, vmem = pltpu.SemaphoreType.DMA, pltpu.VMEM
    hbm = pl.BlockSpec(memory_space=pl.ANY)
    smem = pl.BlockSpec(memory_space=pltpu.SMEM)
    grads = jax.ShapeDtypeStruct((TOK, KVH * HD), F32)
    dq = jax.ShapeDtypeStruct(queries.shape, BF16)
    shares = jax.ShapeDtypeStruct((CHUNKS, 4, 4, CHUNK, HD), BF16)
    places = pl.pallas_call(
        place_kernel, out_shape=jax.ShapeDtypeStruct((3, BLOCKS), jnp.int32), in_specs=[smem], out_specs=smem,
        name="places")(offsets)
    dq_done, shares_done = pl.pallas_call(
        kernel,
        out_shape=(dq, shares),
        in_specs=[smem, hbm, hbm, hbm, hbm],
        out_specs=(hbm, hbm),
        scratch_shapes=[
            vmem((BLOCKS, HALF, HD), BF16), vmem((BLOCKS, HALF, HD), BF16), vmem((TILES, TILE, HD), BF16), vmem((TILES, TILE, HD), BF16),
            vmem((2, ROWS, HD), BF16), vmem((2, ROWS, HD), BF16),
            vmem((SLOTS * TILE, ROWS), F32), vmem((SLOTS * TILE, ROWS), F32), vmem((SLOTS * TILE, ROWS), BF16),
            vmem((SLOTS * TILE_BLOCKS, HALF, HD), F32), vmem((SLOTS * TILE_BLOCKS, HALF, HD), F32), vmem((SLOTS, ROWS, HD), F32),
            vmem((SLOTS, 8, ROWS), F32), vmem((SLOTS, 8, ROWS), F32), vmem((SLOTS, 8, ROWS), F32), vmem((2, 3, 8, ROWS), F32),
            vmem((LAYERS, TOK, HEADS * HD), BF16),
            vmem((2, 2, 4, 2, 2, HALF, HD), BF16),
            vmem((CHUNKS, 4, 2, 2, CHUNK, HD), BF16), vmem((CHUNKS, 4, 2, 2, CHUNK, HD), BF16),
            vmem((CHUNKS, 7, 2, CHUNK, HD), BF16), vmem((CHUNKS, 2, CHUNK, HD), BF16),
            vmem((CHUNKS, 2, 4, CHUNK, HD), BF16), vmem((CHUNKS, 4, 4, CHUNK, HD), BF16),
            dma((2,)), dma((2,)), dma((2, 3)), dma((2, 3, 2)), dma((2, 3, 2)), dma((2, 8, 2)),
            dma((CHUNKS, 2)), dma((CHUNKS, 7, 2)), dma((CHUNKS, 2, 4, 2)), dma((CHUNKS, 3, 2)), dma((1 + CHUNKS,)),
        ],
        compiler_params=pltpu.CompilerParams(collective_id=0, has_side_effects=True, vmem_limit_bytes=58 * 1024 * 1024),
        cost_estimate=pl.CostEstimate(flops=3_400_000_000, bytes_accessed=6_000_000, transcendentals=2_600_000),
        name="attention_backward",
    )(places, queries, grad_out, key_heads.reshape(2, HALF, KVH * HD), value_heads.reshape(2, HALF, KVH * HD))
    return pl.pallas_call(
        write_kernel, grid=(2, SPLIT),
        out_shape=(dq, grads, grads),
        in_specs=[
            pl.BlockSpec((LAYERS, CHUNK, HEADS * HD), lambda half, nth: (0, half * SPLIT + nth, 0)),
            pl.BlockSpec((2, 1, 2, 1, 4, CHUNK, HD), lambda half, nth: (0, nth, 0, half, 0, 0, 0))],
        out_specs=(
            pl.BlockSpec((LAYERS, CHUNK, HEADS * HD), lambda half, nth: (0, half * SPLIT + nth, 0)),
            pl.BlockSpec((CHUNK, KVH * HD), lambda half, nth: (half * SPLIT + nth, 0)),
            pl.BlockSpec((CHUNK, KVH * HD), lambda half, nth: (half * SPLIT + nth, 0))),
        name="write_out",
    )(dq_done, shares_done.reshape(2, SPLIT, 2, 2, 4, CHUNK, HD))


def solution(mesh):
    in_specs = (P(None, "ctx", "kv"), P("ctx", None), P("ctx", None), P(None, "ctx", "kv"), P())
    out_specs = (P(None, "ctx", "kv"), P("ctx", None), P("ctx", None))
    return jax.shard_map(local, mesh=mesh, in_specs=in_specs, out_specs=out_specs, check_vma=False)
```

```python
import jax
import jax.numpy as jnp
from jax import lax
from jax.experimental import pallas as pl
from jax.experimental.pallas import tpu as pltpu
from jax.sharding import PartitionSpec as P

KVH = 8
HD = 128
TOK = 192
HALF = 96
CTX = 16
TOTAL = CTX * TOK
BLOCKS = 2 * CTX
LAYERS = 2
HEADS = 4
UNITS = LAYERS * HEADS
ROWS = UNITS * HALF
TILE = 384
TILE_BLOCKS = TILE // HALF
TILES = TOTAL // TILE
SLOTS = TILES + 1
SPLIT = 2
CHUNK = HALF // SPLIT
CHUNKS = 2 * SPLIT
SCALE = HD ** -0.5
EXP2_SCALE = SCALE * 1.4426950408889634
MESH = pl.DeviceIdType.MESH
BF16 = jnp.bfloat16
F32 = jnp.float32
UNROLL = 3
KEYS, VALUES = 0, 1


def ctx_of(y, z_hi, core):
    return y * 4 + z_hi * 2 + core


def head_of(z_lo, x):
    return z_lo * 2 + x // 2


def kernel(off_ref, q_ref, g_ref, k_ref, v_ref, dq_ref, out_ref,
           rank_of, block_at, stage, all_k, all_v, sorted_k, sorted_v, qs, gs, s_scr, p_scr, d_scr, k_acc, v_acc, q_acc, top_hist, sum_hist, delta_hist, stats, dq_out,
           parts, chip_in, chip_sum, y_in, y_sum, z_in, shares,
           in_sem, own_sem, cross_sem, near_sem, over_sem, mate_sem, chip_sem, y_sem, z_sem, x_sem, out_sem):
    ctx, kv = lax.axis_index("ctx"), lax.axis_index("kv")
    y, z_hi, core, z_lo, x = ctx // 4, (ctx // 2) % 2, ctx % 2, kv // 4, kv % 4
    mate = ctx_of(y, z_hi, 1 - core)
    far = ctx_of(y, 1 - z_hi, core)
    odd = x % 2
    pair = z_lo * 4 + x + 1 - 2 * odd
    y_peers = [ctx_of((y + step) % 4, z_hi, core) for step in (1, 2, 3)]
    x_peers = [z_lo * 4 + (x + step) % 4 for step in (1, 2, 3)]
    z_peers = [(z_lo + step) % 4 * 4 + x for step in (1, 2, 3)]
    at_low, at_high = z_lo == 0, z_lo == 3
    nt_dims = (((1,), (1,)), ((), ()))
    tn_dims = (((0,), (0,)), ((), ()))

    barrier = pltpu.get_barrier_semaphore()
    peers = [(mate, kv)] + [(c, k) for c in y_peers for k in (kv, pair)] + [(ctx, k) for k in x_peers + z_peers]
    peers += [(far, z_idx * 4 + x) for z_idx in range(4)]
    for peer in peers:
        pl.semaphore_signal(barrier, inc=1, device_id=peer, device_id_type=MESH)

    head = head_of(z_lo, x)

    def head_slice(part, head_idx):
        return (k_ref, v_ref)[part].at[:, :, pl.ds(pl.multiple_of(head_idx * HD, HD), HD)]

    def tokens_of(part, ctx_idx):
        return (all_k, all_v)[part].at[pl.ds(2 * ctx_idx, 2)]

    cross_to = [jnp.where(at_low, 2 + nth, nth) for nth in range(2)]
    staged = []
    for part in (KEYS, VALUES):
        staged.append([pltpu.make_async_copy(head_slice(part, head), tokens_of(part, ctx), own_sem.at[part, 0])])
        for nth in range(2):
            staged[part].append(pltpu.make_async_copy(head_slice(part, head_of(cross_to[nth], x)), stage.at[part, nth],
                                                      own_sem.at[part, 1 + nth]))
        for copy in staged[part]:
            copy.start()

    for nth, (ref, dst) in enumerate(((q_ref, qs), (g_ref, gs))):
        for half in range(2):
            for unit in range(UNITS):
                layer, head = divmod(unit, HEADS)
                pltpu.make_async_copy(
                    ref.at[layer, half * HALF:(half + 1) * HALF, head * HD:(head + 1) * HD],
                    dst.at[half, unit * HALF:(unit + 1) * HALF], in_sem.at[nth]).start()


    def rank_step(block, _):
        start = off_ref[block]
        rank = jnp.int32(0)
        for other in range(1, BLOCKS):
            rank += (start >= other * HALF).astype(jnp.int32)
        rank_of[block] = rank
        return 0

    def block_step(rank, _):
        found = jnp.int32(0)
        for block in range(1, BLOCKS):
            found += (off_ref[block] == rank * HALF).astype(jnp.int32) * block
        block_at[rank] = jnp.minimum(found, BLOCKS - 1)
        return 0

    pl.semaphore_wait(barrier, len(peers))

    def describe(src, dst, send_sem, recv_sem, ctx_idx, kv_idx):
        return pltpu.make_async_remote_copy(src_ref=src, dst_ref=dst, send_sem=send_sem, recv_sem=recv_sem,
                                            device_id=(ctx_idx, kv_idx), device_id_type=MESH)

    def remote(src, dst, sems, ctx_idx, kv_idx):
        copy = describe(src, dst, sems.at[0], sems.at[1], ctx_idx, kv_idx)
        copy.start()
        return copy

    def cross(part, act):
        @pl.when(jnp.logical_or(at_low, at_high))
        def _():
            for nth in range(2):
                act(describe(stage.at[part, nth], tokens_of(part, ctx), cross_sem.at[part, 1 + nth], cross_sem.at[part, 0],
                             far, cross_to[nth] * 4 + x))

    near, over, to_mate = {}, {}, {}

    def send_near(part):
        near[part] = [remote(tokens_of(part, ctx), tokens_of(part, ctx), near_sem.at[part, step - 1], y_peers[step - 1], kv)
                      for step in (1, 2, 3)]

    def send_over(part):
        pltpu.make_async_copy(tokens_of(part, far), tokens_of(part, far), cross_sem.at[part, 0]).wait()
        over[part] = [remote(tokens_of(part, far), tokens_of(part, far), over_sem.at[part, step - 1], y_peers[step - 1], kv)
                      for step in (1, 2, 3)]

    def send_mate(part, step, half):
        idx = ctx_of((y - step + 4) % 4, half, core)
        to_mate.setdefault(part, []).append(
            remote(tokens_of(part, idx), tokens_of(part, idx), mate_sem.at[part, len(to_mate.get(part, []))], mate, kv))

    for part in (KEYS, VALUES):
        for copy in staged[part]:
            copy.wait()
    cross(KEYS, lambda copy: copy.start())
    send_near(KEYS)
    cross(KEYS, lambda copy: copy.wait_send())
    cross(VALUES, lambda copy: copy.start())
    send_mate(KEYS, 0, z_hi)
    for copy in near[KEYS]:
        copy.wait_send()
    send_near(VALUES)
    send_mate(VALUES, 0, z_hi)
    lax.fori_loop(0, BLOCKS, block_step, 0)
    send_over(KEYS)
    send_mate(KEYS, 0, 1 - z_hi)
    for step in (1, 3, 2):
        near[KEYS][step - 1].wait_recv()
        send_mate(KEYS, step, z_hi)
    send_over(VALUES)
    send_mate(VALUES, 0, 1 - z_hi)
    lax.fori_loop(0, BLOCKS, rank_step, 0)
    for step in (1, 3, 2):
        over[KEYS][step - 1].wait_recv()
        send_mate(KEYS, step, 1 - z_hi)
    for step in (1, 3, 2):
        near[VALUES][step - 1].wait_recv()
        send_mate(VALUES, step, z_hi)
    for copy in to_mate[KEYS]:
        copy.wait_recv()

    def sort(part):
        for rank in range(BLOCKS):
            first = rank % TILE_BLOCKS * HALF
            (sorted_k, sorted_v)[part][rank // TILE_BLOCKS, first:first + HALF] = (all_k, all_v)[part][block_at[rank]]

    sort(KEYS)
    pltpu.make_async_copy(qs, qs, in_sem.at[0]).wait()
    pltpu.make_async_copy(gs, gs, in_sem.at[1]).wait()

    start_0, start_1 = off_ref[2 * ctx], off_ref[2 * ctx + 1]
    count_0 = sum(((start_0 >= tile * TILE).astype(jnp.int32) for tile in range(1, TILES)), jnp.int32(1))
    count_1 = SLOTS - count_0

    def slot_of(slot):
        half = (slot >= count_0).astype(jnp.int32)
        tile = slot - count_0 * half
        return half, tile, tile, pl.ds(pl.multiple_of(slot * TILE, TILE), TILE)

    def carried(slot):
        return (slot != count_0).astype(F32)

    def fold(tile, op):
        return op(tile.reshape(TILE // 8, 8, ROWS), axis=0)

    def score_step(slot, top):
        half, tile, keys, rows = slot_of(slot)
        s = lax.dot_general(sorted_k[keys], qs[half], nt_dims, preferred_element_type=F32)
        ahead = lax.broadcasted_iota(jnp.int32, (TILE, ROWS), 0) - lax.broadcasted_iota(jnp.int32, (TILE, ROWS), 1) % HALF
        s = jnp.where(ahead <= start_0 + (start_1 - start_0) * half - tile * TILE, s, -1e30)
        s_scr[rows] = s
        keep = carried(slot)
        top = jnp.maximum(top * keep - 1e30 * (1.0 - keep), fold(s, jnp.max))
        top_hist[slot] = top
        return top

    top = lax.fori_loop(0, SLOTS - UNROLL, score_step, jnp.full((8, ROWS), -1e30, F32), unroll=UNROLL)
    for step in (1, 3, 2):
        over[VALUES][step - 1].wait_recv()
        send_mate(VALUES, step, 1 - z_hi)
    lax.fori_loop(SLOTS - UNROLL, SLOTS, score_step, top, unroll=UNROLL)
    for half, last in enumerate((count_0 - 1, SLOTS - 1)):
        stats[half, 0] = jnp.broadcast_to(jnp.max(top_hist[last], axis=0, keepdims=True), (8, ROWS))
    for copy in to_mate[VALUES]:
        copy.wait_recv()
    sort(VALUES)

    def sum_step(slot, sums):
        half, tile, keys, rows = slot_of(slot)
        weight = jnp.exp2((s_scr[rows] - stats[half, 0][:1]) * EXP2_SCALE)
        grad_prob = lax.dot_general(sorted_v[keys], gs[half], nt_dims, preferred_element_type=F32)
        s_scr[rows] = weight
        p_scr[rows] = grad_prob
        keep = carried(slot)
        total, delta = sums[0] * keep + fold(weight, jnp.sum), sums[1] * keep + fold(weight * grad_prob, jnp.sum)
        sum_hist[slot], delta_hist[slot] = total, delta
        return total, delta

    zero = jnp.zeros((8, ROWS), F32)
    lax.fori_loop(0, SLOTS, sum_step, (zero, zero), unroll=UNROLL)
    for half, last in enumerate((count_0 - 1, SLOTS - 1)):
        inv = 1.0 / jnp.sum(sum_hist[last], axis=0, keepdims=True)
        delta = jnp.sum(delta_hist[last], axis=0, keepdims=True) * inv
        stats[half, 1] = jnp.broadcast_to(inv, (8, ROWS))
        stats[half, 2] = jnp.broadcast_to(delta, (8, ROWS))

    def value_step(slot, _):
        half, tile, keys, rows = slot_of(slot)
        prob = s_scr[rows] * stats[half, 1][:1]
        v_acc[pl.ds(slot * TILE_BLOCKS, TILE_BLOCKS)] = jnp.dot(prob.astype(BF16), gs[half], preferred_element_type=F32).reshape(TILE_BLOCKS, HALF, HD)
        d_scr[rows] = (prob * (p_scr[rows] - stats[half, 2][:1])).astype(BF16)
        return 0

    def key_step(slot, _):
        half, tile, keys, rows = slot_of(slot)
        k_acc[pl.ds(slot * TILE_BLOCKS, TILE_BLOCKS)] = jnp.dot(d_scr[rows], qs[half], preferred_element_type=F32).reshape(TILE_BLOCKS, HALF, HD)
        return 0

    def query_step(slot, _):
        half, tile, keys, rows = slot_of(slot)
        term = lax.dot_general(d_scr[rows], sorted_k[keys], tn_dims, preferred_element_type=F32)
        q_acc[slot] = term + q_acc[jnp.maximum(slot - 1, 0)] * carried(slot)
        return 0

    def by_tokens(part, acc, scale):
        for block in range(BLOCKS):
            rank = rank_of[block]
            in_0 = (rank < count_0 * TILE_BLOCKS).astype(jnp.int32)
            in_1 = (rank < count_1 * TILE_BLOCKS).astype(jnp.int32)
            both = (acc[rank * in_0] * (in_0.astype(F32) * scale)
                    + acc[(count_0 * TILE_BLOCKS + rank) * in_1] * (in_1.astype(F32) * scale))
            parts[part, block // 2 % 2, block // 8, block % 2, block // 4 % 2] = both.astype(BF16)

    chunks = {KEYS: range(SPLIT), VALUES: range(SPLIT, CHUNKS)}
    chip, along, along_z, along_x = {}, {}, {}, {}

    def rows_of(chunk):
        return slice(chunk % SPLIT * CHUNK, (chunk % SPLIT + 1) * CHUNK)

    def send_chip(part):
        for chunk in chunks[part]:
            chip[chunk] = remote(parts.at[part, 1 - core, :, :, :, rows_of(chunk)], chip_in.at[chunk], chip_sem.at[chunk], mate, kv)

    def send_y(part):
        for chunk in chunks[part]:
            chip[chunk].wait_recv()
            along[chunk] = []
            for step in (2, 1, 3, 0):
                to_y = (y + step) % 4
                both = parts[part, core, to_y, :, :, rows_of(chunk)].astype(F32) + chip_in[chunk, to_y].astype(F32)
                chip_sum[chunk, step] = both.astype(BF16)
                to_ctx = y_peers[step - 1] if step else ctx
                for other in ((1, 0) if step else (1,)):
                    nth = 2 * step + other - 1
                    along[chunk].append(remote(chip_sum.at[chunk, step, 1 - odd if other else odd], y_in.at[chunk, nth],
                                               y_sem.at[chunk, nth], to_ctx, pair if other else kv))

    def send_z(part):
        for chunk in chunks[part]:
            for copy in along[chunk]:
                copy.wait_recv()
            total = chip_sum[chunk, 0, odd].astype(F32)
            for nth in range(7):
                total += y_in[chunk, nth].astype(F32)
            y_sum[chunk] = total.astype(BF16)
            along_z[chunk] = [
                remote(y_sum.at[chunk, 1 - z_hi], z_in.at[chunk, 1, z_lo], z_sem.at[chunk, 1, step], far, (z_lo + step) % 4 * 4 + x)
                for step in (0, 3, 1, 2)]
            along_z[chunk] += [
                remote(y_sum.at[chunk, z_hi], z_in.at[chunk, 0, z_lo], z_sem.at[chunk, 0, step], ctx, z_peers[step - 1])
                for step in (3, 2, 1)]
            z_in[chunk, 0, z_lo] = y_sum[chunk, z_hi]

    def send_x(part):
        for chunk in chunks[part]:
            for copy in along_z[chunk]:
                copy.wait_recv()
            shares[chunk, x] = (z_in[chunk, 0].astype(F32) + z_in[chunk, 1].astype(F32)).astype(BF16)
            slot = shares.at[chunk, x]
            along_x[chunk] = [remote(slot, slot, x_sem.at[chunk, step - 1], ctx, x_peers[step - 1]) for step in (2, 1, 3)]

    written = []

    def finish(part):
        for chunk in chunks[part]:
            for copy in along_x[chunk]:
                copy.wait_recv()
            written.append(pltpu.make_async_copy(shares.at[chunk], out_ref.at[chunk], out_sem.at[1 + chunk]))
            written[-1].start()

    lax.fori_loop(0, SLOTS, value_step, 0, unroll=UNROLL)
    by_tokens(VALUES, v_acc, 1.0)
    send_chip(VALUES)
    lax.fori_loop(0, SLOTS, key_step, 0, unroll=UNROLL)
    send_y(VALUES)
    by_tokens(KEYS, k_acc, SCALE)
    send_chip(KEYS)
    q_acc[0] = jnp.zeros((ROWS, HD), F32)
    lax.fori_loop(0, 4, query_step, 0)
    send_y(KEYS)
    lax.fori_loop(4, 7, query_step, 0)
    send_z(VALUES)
    lax.fori_loop(7, SLOTS, query_step, 0)
    for half in range(2):
        last = count_0 - 1 if half == 0 else SLOTS - 1
        for unit in range(UNITS):
            layer, head_idx = divmod(unit, HEADS)
            dq_out[layer, half * HALF:(half + 1) * HALF, head_idx * HD:(head_idx + 1) * HD] = (
                q_acc[last, unit * HALF:(unit + 1) * HALF] * SCALE).astype(BF16)
    written.append(pltpu.make_async_copy(dq_out, dq_ref, out_sem.at[0]))
    written[-1].start()
    send_z(KEYS)
    send_x(VALUES)
    send_x(KEYS)
    finish(VALUES)
    finish(KEYS)
    for copy in written:
        copy.wait()
    cross(VALUES, lambda copy: copy.wait_send())
    for copy in near[VALUES]:
        copy.wait_send()
    for group in (over, to_mate, along, along_z, along_x):
        for copies in group.values():
            for copy in copies:
                copy.wait_send()
    for copy in chip.values():
        copy.wait_send()


def write_kernel(dq_in, share_in, dq_ref, gk_ref, gv_ref, dq_buf, shares, grads, in_sem, out_sem):
    dq_load = pltpu.make_async_copy(dq_in, dq_buf, in_sem.at[CHUNKS])
    loads = [pltpu.make_async_copy(share_in.at[chunk], shares.at[chunk], in_sem.at[chunk]) for chunk in range(CHUNKS)]
    for copy in loads + [dq_load]:
        copy.start()
    stores = []

    def store(src, dst):
        stores.append(pltpu.make_async_copy(src, dst, out_sem.at[len(stores)]))
        stores[-1].start()

    for part, ref in ((KEYS, gk_ref), (VALUES, gv_ref)):
        for nth in range(SPLIT):
            chunk = part * SPLIT + nth
            loads[chunk].wait()
            for half in range(2):
                rows = slice(half * HALF + nth * CHUNK, half * HALF + (nth + 1) * CHUNK)
                for x in (half, half + 2):
                    for z_lo in range(4):
                        col = head_of(z_lo, x) * HD
                        grads[part, rows, col:col + HD] = shares[chunk, x, z_lo].astype(F32)
                store(grads.at[part, rows], ref.at[rows])
    dq_load.wait()
    store(dq_buf, dq_ref)
    for copy in stores:
        copy.wait()


def local(queries, key_heads, value_heads, grad_out, offsets):
    dma, vmem = pltpu.SemaphoreType.DMA, pltpu.VMEM
    hbm = pl.BlockSpec(memory_space=pl.ANY)
    smem = pl.BlockSpec(memory_space=pltpu.SMEM)
    grads = jax.ShapeDtypeStruct((TOK, KVH * HD), F32)
    dq = jax.ShapeDtypeStruct(queries.shape, BF16)
    shares = jax.ShapeDtypeStruct((CHUNKS, 4, 4, CHUNK, HD), BF16)
    dq_done, shares_done = pl.pallas_call(
        kernel,
        out_shape=(dq, shares),
        in_specs=[smem, hbm, hbm, hbm, hbm],
        out_specs=(hbm, hbm),
        scratch_shapes=[
            pltpu.SMEM((BLOCKS,), jnp.int32), pltpu.SMEM((BLOCKS,), jnp.int32), vmem((2, 2, 2, HALF, HD), BF16),
            vmem((BLOCKS, HALF, HD), BF16), vmem((BLOCKS, HALF, HD), BF16), vmem((TILES, TILE, HD), BF16), vmem((TILES, TILE, HD), BF16),
            vmem((2, ROWS, HD), BF16), vmem((2, ROWS, HD), BF16),
            vmem((SLOTS * TILE, ROWS), F32), vmem((SLOTS * TILE, ROWS), F32), vmem((SLOTS * TILE, ROWS), BF16),
            vmem((SLOTS * TILE_BLOCKS, HALF, HD), F32), vmem((SLOTS * TILE_BLOCKS, HALF, HD), F32), vmem((SLOTS, ROWS, HD), F32),
            vmem((SLOTS, 8, ROWS), F32), vmem((SLOTS, 8, ROWS), F32), vmem((SLOTS, 8, ROWS), F32), vmem((2, 3, 8, ROWS), F32),
            vmem((LAYERS, TOK, HEADS * HD), BF16),
            vmem((2, 2, 4, 2, 2, HALF, HD), BF16),
            vmem((CHUNKS, 4, 2, 2, CHUNK, HD), BF16), vmem((CHUNKS, 4, 2, 2, CHUNK, HD), BF16),
            vmem((CHUNKS, 7, 2, CHUNK, HD), BF16), vmem((CHUNKS, 2, CHUNK, HD), BF16),
            vmem((CHUNKS, 2, 4, CHUNK, HD), BF16), vmem((CHUNKS, 4, 4, CHUNK, HD), BF16),
            dma((2,)), dma((2, 3)), dma((2, 3)), dma((2, 3, 2)), dma((2, 3, 2)), dma((2, 8, 2)),
            dma((CHUNKS, 2)), dma((CHUNKS, 7, 2)), dma((CHUNKS, 2, 4, 2)), dma((CHUNKS, 3, 2)), dma((1 + CHUNKS,)),
        ],
        compiler_params=pltpu.CompilerParams(collective_id=0, has_side_effects=True, vmem_limit_bytes=58 * 1024 * 1024),
        cost_estimate=pl.CostEstimate(flops=3_400_000_000, bytes_accessed=6_000_000, transcendentals=2_600_000),
        name="attention_backward",
    )(offsets, queries, grad_out, key_heads.reshape(2, HALF, KVH * HD), value_heads.reshape(2, HALF, KVH * HD))
    return pl.pallas_call(
        write_kernel,
        out_shape=(dq, grads, grads),
        in_specs=[hbm, hbm],
        out_specs=(hbm, hbm, hbm),
        scratch_shapes=[vmem(queries.shape, BF16), vmem(shares.shape, BF16), vmem((2, TOK, KVH * HD), F32),
                        dma((CHUNKS + 1,)), dma((2 * CHUNKS + 1,))],
        compiler_params=pltpu.CompilerParams(vmem_limit_bytes=58 * 1024 * 1024),
        name="write_out",
    )(dq_done, shares_done)


def solution(mesh):
    in_specs = (P(None, "ctx", "kv"), P("ctx", None), P("ctx", None), P(None, "ctx", "kv"), P())
    out_specs = (P(None, "ctx", "kv"), P("ctx", None), P("ctx", None))
    return jax.shard_map(local, mesh=mesh, in_specs=in_specs, out_specs=out_specs, check_vma=False)
```

```python
import jax
import jax.numpy as jnp
from jax import lax
from jax.experimental import pallas as pl
from jax.experimental.pallas import tpu as pltpu
from jax.sharding import PartitionSpec as P

KVH = 8
HD = 128
TOK = 192
HALF = 96
CTX = 16
TOTAL = CTX * TOK
BLOCKS = 2 * CTX
LAYERS = 2
HEADS = 4
UNITS = LAYERS * HEADS
ROWS = UNITS * HALF
TILE = 384
TILE_BLOCKS = TILE // HALF
TILES = TOTAL // TILE
SLOTS = TILES + 1
SPLIT = 2
CHUNK = HALF // SPLIT
CHUNKS = 2 * SPLIT
SCALE = HD ** -0.5
EXP2_SCALE = SCALE * 1.4426950408889634
MESH = pl.DeviceIdType.MESH
BF16 = jnp.bfloat16
F32 = jnp.float32
UNROLL = 3
KEYS, VALUES = 0, 1


def ctx_of(y, z_hi, core):
    return y * 4 + z_hi * 2 + core


def head_of(z_lo, x):
    return z_lo * 2 + x // 2


def kernel(off_ref, q_ref, g_ref, k_ref, v_ref, dq_ref, out_ref,
           rank_of, block_at, stage, all_k, all_v, sorted_k, sorted_v, qs, gs, s_scr, p_scr, d_scr, k_acc, v_acc, q_acc, top_hist, sum_hist, delta_hist, stats, dq_out,
           parts, chip_in, chip_sum, y_in, y_sum, z_in, shares,
           in_sem, own_sem, cross_sem, near_sem, over_sem, mate_sem, chip_sem, y_sem, z_sem, x_sem, out_sem):
    ctx, kv = lax.axis_index("ctx"), lax.axis_index("kv")
    y, z_hi, core, z_lo, x = ctx // 4, (ctx // 2) % 2, ctx % 2, kv // 4, kv % 4
    mate = ctx_of(y, z_hi, 1 - core)
    far = ctx_of(y, 1 - z_hi, core)
    odd = x % 2
    pair = z_lo * 4 + x + 1 - 2 * odd
    y_peers = [ctx_of((y + step) % 4, z_hi, core) for step in (1, 2, 3)]
    x_peers = [z_lo * 4 + (x + step) % 4 for step in (1, 2, 3)]
    z_peers = [(z_lo + step) % 4 * 4 + x for step in (1, 2, 3)]
    at_low, at_high = z_lo == 0, z_lo == 3
    nt_dims = (((1,), (1,)), ((), ()))
    tn_dims = (((0,), (0,)), ((), ()))

    barrier = pltpu.get_barrier_semaphore()
    peers = [(far, z_idx * 4 + x) for z_idx in range(4)] + [(mate, kv)] + [(c, k) for c in y_peers for k in (kv, pair)] + [(ctx, k) for k in x_peers + z_peers]
    for peer in peers:
        pl.semaphore_signal(barrier, inc=1, device_id=peer, device_id_type=MESH)

    head = head_of(z_lo, x)

    def head_slice(part, head_idx):
        return (k_ref, v_ref)[part].at[:, :, pl.ds(pl.multiple_of(head_idx * HD, HD), HD)]

    def tokens_of(part, ctx_idx):
        return (all_k, all_v)[part].at[ctx_idx // 4, ctx_idx // 2 % 2, ctx_idx % 2]

    cross_to = [jnp.where(at_low, 2 + nth, nth) for nth in range(2)]
    staged = []
    for part in (KEYS, VALUES):
        staged.append([pltpu.make_async_copy(head_slice(part, head), tokens_of(part, ctx), own_sem.at[part, 0])])
        for nth in range(2):
            staged[part].append(pltpu.make_async_copy(head_slice(part, head_of(cross_to[nth], x)), stage.at[part, nth],
                                                      own_sem.at[part, 1 + nth]))
        for copy in staged[part]:
            copy.start()

    def rank_step(block, _):
        start = off_ref[block]
        rank = jnp.int32(0)
        for other in range(1, BLOCKS):
            rank += (start >= other * HALF).astype(jnp.int32)
        rank_of[block] = rank
        return 0

    def block_step(rank, _):
        found = jnp.int32(0)
        for block in range(1, BLOCKS):
            found += (off_ref[block] == rank * HALF).astype(jnp.int32) * block
        block_at[rank] = jnp.minimum(found, BLOCKS - 1)
        return 0

    pl.semaphore_wait(barrier, len(peers))

    def describe(src, dst, send_sem, recv_sem, ctx_idx, kv_idx):
        return pltpu.make_async_remote_copy(src_ref=src, dst_ref=dst, send_sem=send_sem, recv_sem=recv_sem,
                                            device_id=(ctx_idx, kv_idx), device_id_type=MESH)

    def remote(src, dst, sems, ctx_idx, kv_idx):
        copy = describe(src, dst, sems.at[0], sems.at[1], ctx_idx, kv_idx)
        copy.start()
        return copy

    def cross(part, act):
        @pl.when(jnp.logical_or(at_low, at_high))
        def _():
            for nth in range(2):
                act(describe(stage.at[part, nth], tokens_of(part, ctx), cross_sem.at[part, 1 + nth], cross_sem.at[part, 0],
                             far, cross_to[nth] * 4 + x))

    near, over, to_mate = {}, {}, {}

    def send_near(part):
        near[part] = [remote(tokens_of(part, ctx), tokens_of(part, ctx), near_sem.at[part, step - 1], y_peers[step - 1], kv)
                      for step in (1, 2, 3)]

    def send_over(part):
        pltpu.make_async_copy(tokens_of(part, far), tokens_of(part, far), cross_sem.at[part, 0]).wait()
        over[part] = [remote(tokens_of(part, far), tokens_of(part, far), over_sem.at[part, step - 1], y_peers[step - 1], kv)
                      for step in (1, 2, 3)]

    def send_mate(part, half):
        src = (all_k, all_v)[part].at[:, half, core]
        to_mate.setdefault(part, []).append(remote(src, src, mate_sem.at[part, len(to_mate.get(part, []))], mate, kv))

    for copy in staged[KEYS]:
        copy.wait()
    cross(KEYS, lambda copy: copy.start())
    send_near(KEYS)
    for nth, (ref, dst) in enumerate(((q_ref, qs), (g_ref, gs))):
        for half in range(2):
            for unit in range(UNITS):
                layer, head = divmod(unit, HEADS)
                pltpu.make_async_copy(
                    ref.at[layer, half * HALF:(half + 1) * HALF, head * HD:(head + 1) * HD],
                    dst.at[half, unit * HALF:(unit + 1) * HALF], in_sem.at[nth]).start()
    for copy in staged[VALUES]:
        copy.wait()
    cross(KEYS, lambda copy: copy.wait_send())
    cross(VALUES, lambda copy: copy.start())
    for copy in near[KEYS]:
        copy.wait_send()
    send_near(VALUES)
    lax.fori_loop(0, BLOCKS, block_step, 0)
    send_over(KEYS)
    for copy in near[KEYS]:
        copy.wait_recv()
    send_mate(KEYS, z_hi)
    send_over(VALUES)
    lax.fori_loop(0, BLOCKS, rank_step, 0)
    for copy in over[KEYS]:
        copy.wait_recv()
    send_mate(KEYS, 1 - z_hi)
    for copy in near[VALUES]:
        copy.wait_recv()
    send_mate(VALUES, z_hi)
    for copy in to_mate[KEYS]:
        copy.wait_recv()

    by_block = [ref.reshape(BLOCKS, HALF, HD) for ref in (all_k, all_v)]

    def sort(part):
        for rank in range(BLOCKS):
            first = rank % TILE_BLOCKS * HALF
            (sorted_k, sorted_v)[part][rank // TILE_BLOCKS, first:first + HALF] = by_block[part][block_at[rank]]

    sort(KEYS)
    pltpu.make_async_copy(qs, qs, in_sem.at[0]).wait()
    pltpu.make_async_copy(gs, gs, in_sem.at[1]).wait()

    start_0, start_1 = off_ref[2 * ctx], off_ref[2 * ctx + 1]
    count_0 = sum(((start_0 >= tile * TILE).astype(jnp.int32) for tile in range(1, TILES)), jnp.int32(1))
    count_1 = SLOTS - count_0

    def slot_of(slot):
        half = (slot >= count_0).astype(jnp.int32)
        tile = slot - count_0 * half
        return half, tile, tile, pl.ds(pl.multiple_of(slot * TILE, TILE), TILE)

    def carried(slot):
        return (slot != count_0).astype(F32)

    def fold(tile, op):
        return op(tile.reshape(TILE // 8, 8, ROWS), axis=0)

    def score_step(slot, top):
        half, tile, keys, rows = slot_of(slot)
        s = lax.dot_general(sorted_k[keys], qs[half], nt_dims, preferred_element_type=F32)
        ahead = lax.broadcasted_iota(jnp.int32, (TILE, ROWS), 0) - lax.broadcasted_iota(jnp.int32, (TILE, ROWS), 1) % HALF
        s = jnp.where(ahead <= start_0 + (start_1 - start_0) * half - tile * TILE, s, -1e30)
        s_scr[rows] = s
        keep = carried(slot)
        top = jnp.maximum(top * keep - 1e30 * (1.0 - keep), fold(s, jnp.max))
        top_hist[slot] = top
        return top

    top = lax.fori_loop(0, SLOTS - UNROLL, score_step, jnp.full((8, ROWS), -1e30, F32), unroll=UNROLL)
    for copy in over[VALUES]:
        copy.wait_recv()
    send_mate(VALUES, 1 - z_hi)
    lax.fori_loop(SLOTS - UNROLL, SLOTS, score_step, top, unroll=UNROLL)
    for half, last in enumerate((count_0 - 1, SLOTS - 1)):
        stats[half, 0] = jnp.broadcast_to(jnp.max(top_hist[last], axis=0, keepdims=True), (8, ROWS))
    for copy in to_mate[VALUES]:
        copy.wait_recv()
    sort(VALUES)

    def sum_step(slot, sums):
        half, tile, keys, rows = slot_of(slot)
        weight = jnp.exp2((s_scr[rows] - stats[half, 0][:1]) * EXP2_SCALE)
        grad_prob = lax.dot_general(sorted_v[keys], gs[half], nt_dims, preferred_element_type=F32)
        s_scr[rows] = weight
        p_scr[rows] = grad_prob
        keep = carried(slot)
        total, delta = sums[0] * keep + fold(weight, jnp.sum), sums[1] * keep + fold(weight * grad_prob, jnp.sum)
        sum_hist[slot], delta_hist[slot] = total, delta
        return total, delta

    zero = jnp.zeros((8, ROWS), F32)
    lax.fori_loop(0, SLOTS, sum_step, (zero, zero), unroll=UNROLL)
    for half, last in enumerate((count_0 - 1, SLOTS - 1)):
        inv = 1.0 / jnp.sum(sum_hist[last], axis=0, keepdims=True)
        delta = jnp.sum(delta_hist[last], axis=0, keepdims=True) * inv
        stats[half, 1] = jnp.broadcast_to(inv, (8, ROWS))
        stats[half, 2] = jnp.broadcast_to(delta, (8, ROWS))

    def value_step(slot, _):
        half, tile, keys, rows = slot_of(slot)
        prob = s_scr[rows] * stats[half, 1][:1]
        v_acc[pl.ds(slot * TILE_BLOCKS, TILE_BLOCKS)] = jnp.dot(prob.astype(BF16), gs[half], preferred_element_type=F32).reshape(TILE_BLOCKS, HALF, HD)
        d_scr[rows] = (prob * (p_scr[rows] - stats[half, 2][:1])).astype(BF16)
        return 0

    def key_step(slot, _):
        half, tile, keys, rows = slot_of(slot)
        k_acc[pl.ds(slot * TILE_BLOCKS, TILE_BLOCKS)] = jnp.dot(d_scr[rows], qs[half], preferred_element_type=F32).reshape(TILE_BLOCKS, HALF, HD)
        return 0

    def query_step(slot, _):
        half, tile, keys, rows = slot_of(slot)
        term = lax.dot_general(d_scr[rows], sorted_k[keys], tn_dims, preferred_element_type=F32)
        q_acc[slot] = term + q_acc[jnp.maximum(slot - 1, 0)] * carried(slot)
        return 0

    def by_tokens(part, acc, scale):
        for block in range(BLOCKS):
            rank = rank_of[block]
            in_0 = (rank < count_0 * TILE_BLOCKS).astype(jnp.int32)
            in_1 = (rank < count_1 * TILE_BLOCKS).astype(jnp.int32)
            both = (acc[rank * in_0] * (in_0.astype(F32) * scale)
                    + acc[(count_0 * TILE_BLOCKS + rank) * in_1] * (in_1.astype(F32) * scale))
            parts[part, block // 2 % 2, block // 8, block % 2, block // 4 % 2] = both.astype(BF16)

    chunks = {KEYS: range(SPLIT), VALUES: range(SPLIT, CHUNKS)}
    chip, along, along_z, along_x, written = {}, {}, {}, {}, []

    def rows_of(chunk):
        return slice(chunk % SPLIT * CHUNK, (chunk % SPLIT + 1) * CHUNK)

    def send_chip(part):
        for chunk in chunks[part]:
            chip[chunk] = remote(parts.at[part, 1 - core, :, :, :, rows_of(chunk)], chip_in.at[chunk], chip_sem.at[chunk], mate, kv)

    def send_y(part):
        for chunk in chunks[part]:
            chip[chunk].wait_recv()
            along[chunk] = []
            for step in (2, 1, 3, 0):
                to_y = (y + step) % 4
                both = parts[part, core, to_y, :, :, rows_of(chunk)].astype(F32) + chip_in[chunk, to_y].astype(F32)
                chip_sum[chunk, step] = both.astype(BF16)
                to_ctx = y_peers[step - 1] if step else ctx
                for other in ((1, 0) if step else (1,)):
                    nth = 2 * step + other - 1
                    along[chunk].append(remote(chip_sum.at[chunk, step, 1 - odd if other else odd], y_in.at[chunk, nth],
                                               y_sem.at[chunk, nth], to_ctx, pair if other else kv))

    def send_z(part):
        for chunk in chunks[part]:
            for copy in along[chunk]:
                copy.wait_recv()
            total = chip_sum[chunk, 0, odd].astype(F32)
            for nth in range(7):
                total += y_in[chunk, nth].astype(F32)
            y_sum[chunk] = total.astype(BF16)
            along_z[chunk] = [
                remote(y_sum.at[chunk, 1 - z_hi], z_in.at[chunk, 1, z_lo], z_sem.at[chunk, 1, step], far, (z_lo + step) % 4 * 4 + x)
                for step in (0, 3, 1, 2)]
            along_z[chunk] += [
                remote(y_sum.at[chunk, z_hi], z_in.at[chunk, 0, z_lo], z_sem.at[chunk, 0, step], ctx, z_peers[step - 1])
                for step in (3, 2, 1)]
            z_in[chunk, 0, z_lo] = y_sum[chunk, z_hi]

    def send_x(part):
        for chunk in chunks[part]:
            for copy in along_z[chunk]:
                copy.wait_recv()
            shares[chunk] = (z_in[chunk, 0].astype(F32) + z_in[chunk, 1].astype(F32)).astype(BF16)
            src, dst = shares.at[chunk], out_ref.at[chunk, x]
            along_x[chunk] = [remote(src, dst, x_sem.at[chunk, step - 1], ctx, x_peers[step - 1]) for step in (2, 1, 3)]
            written.append(pltpu.make_async_copy(src, dst, out_sem.at[1 + chunk]))
            written[-1].start()

    lax.fori_loop(0, SLOTS, value_step, 0, unroll=SLOTS)
    by_tokens(VALUES, v_acc, 1.0)
    send_chip(VALUES)
    lax.fori_loop(0, SLOTS, key_step, 0, unroll=UNROLL)
    send_y(VALUES)
    by_tokens(KEYS, k_acc, SCALE)
    send_chip(KEYS)
    q_acc[0] = jnp.zeros((ROWS, HD), F32)
    lax.fori_loop(0, 4, query_step, 0)
    send_y(KEYS)
    lax.fori_loop(4, 7, query_step, 0)
    send_z(VALUES)
    lax.fori_loop(7, SLOTS, query_step, 0)
    for half in range(2):
        last = count_0 - 1 if half == 0 else SLOTS - 1
        for unit in range(UNITS):
            layer, head_idx = divmod(unit, HEADS)
            dq_out[layer, half * HALF:(half + 1) * HALF, head_idx * HD:(head_idx + 1) * HD] = (
                q_acc[last, unit * HALF:(unit + 1) * HALF] * SCALE).astype(BF16)
    written.append(pltpu.make_async_copy(dq_out, dq_ref, out_sem.at[0]))
    written[-1].start()
    send_z(KEYS)
    send_x(VALUES)
    send_x(KEYS)
    cross(VALUES, lambda copy: copy.wait_send())
    for copy in near[VALUES] + list(chip.values()):
        copy.wait_send()
    for group in (over, to_mate, along, along_z):
        for copies in group.values():
            for copy in copies:
                copy.wait_send()
    for copy in written:
        copy.wait()
    for part in (VALUES, KEYS):
        for chunk in chunks[part]:
            for copy in along_x[chunk]:
                copy.wait()


def write_kernel(dq_in, share_in, dq_ref, gk_ref, gv_ref, dq_buf, shares, grads, in_sem, out_sem):
    dq_load = pltpu.make_async_copy(dq_in, dq_buf, in_sem.at[CHUNKS])
    loads = [pltpu.make_async_copy(share_in.at[chunk], shares.at[chunk], in_sem.at[chunk]) for chunk in range(CHUNKS)]
    for copy in loads + [dq_load]:
        copy.start()
    stores = []

    def store(src, dst):
        stores.append(pltpu.make_async_copy(src, dst, out_sem.at[len(stores)]))
        stores[-1].start()

    for part, ref in ((KEYS, gk_ref), (VALUES, gv_ref)):
        for nth in range(SPLIT):
            chunk = part * SPLIT + nth
            loads[chunk].wait()
            for half in range(2):
                rows = slice(half * HALF + nth * CHUNK, half * HALF + (nth + 1) * CHUNK)
                for x in (half, half + 2):
                    for z_lo in range(4):
                        col = head_of(z_lo, x) * HD
                        grads[part, rows, col:col + HD] = shares[chunk, x, z_lo].astype(F32)
                store(grads.at[part, rows], ref.at[rows])
    dq_load.wait()
    store(dq_buf, dq_ref)
    for copy in stores:
        copy.wait()


def local(queries, key_heads, value_heads, grad_out, offsets):
    dma, vmem = pltpu.SemaphoreType.DMA, pltpu.VMEM
    hbm = pl.BlockSpec(memory_space=pl.ANY)
    smem = pl.BlockSpec(memory_space=pltpu.SMEM)
    grads = jax.ShapeDtypeStruct((TOK, KVH * HD), F32)
    dq = jax.ShapeDtypeStruct(queries.shape, BF16)
    shares = jax.ShapeDtypeStruct((CHUNKS, 4, 4, CHUNK, HD), BF16)
    dq_done, shares_done = pl.pallas_call(
        kernel,
        out_shape=(dq, shares),
        in_specs=[smem, hbm, hbm, hbm, hbm],
        out_specs=(hbm, hbm),
        scratch_shapes=[
            pltpu.SMEM((BLOCKS,), jnp.int32), pltpu.SMEM((BLOCKS,), jnp.int32), vmem((2, 2, 2, HALF, HD), BF16),
            vmem((4, 2, 2, 2, HALF, HD), BF16), vmem((4, 2, 2, 2, HALF, HD), BF16), vmem((TILES, TILE, HD), BF16), vmem((TILES, TILE, HD), BF16),
            vmem((2, ROWS, HD), BF16), vmem((2, ROWS, HD), BF16),
            vmem((SLOTS * TILE, ROWS), F32), vmem((SLOTS * TILE, ROWS), F32), vmem((SLOTS * TILE, ROWS), BF16),
            vmem((SLOTS * TILE_BLOCKS, HALF, HD), F32), vmem((SLOTS * TILE_BLOCKS, HALF, HD), F32), vmem((SLOTS, ROWS, HD), F32),
            vmem((SLOTS, 8, ROWS), F32), vmem((SLOTS, 8, ROWS), F32), vmem((SLOTS, 8, ROWS), F32), vmem((2, 3, 8, ROWS), F32),
            vmem((LAYERS, TOK, HEADS * HD), BF16),
            vmem((2, 2, 4, 2, 2, HALF, HD), BF16),
            vmem((CHUNKS, 4, 2, 2, CHUNK, HD), BF16), vmem((CHUNKS, 4, 2, 2, CHUNK, HD), BF16),
            vmem((CHUNKS, 7, 2, CHUNK, HD), BF16), vmem((CHUNKS, 2, CHUNK, HD), BF16),
            vmem((CHUNKS, 2, 4, CHUNK, HD), BF16), vmem((CHUNKS, 4, CHUNK, HD), BF16),
            dma((2,)), dma((2, 3)), dma((2, 3)), dma((2, 3, 2)), dma((2, 3, 2)), dma((2, 2, 2)),
            dma((CHUNKS, 2)), dma((CHUNKS, 7, 2)), dma((CHUNKS, 2, 4, 2)), dma((CHUNKS, 3, 2)), dma((1 + CHUNKS,)),
        ],
        compiler_params=pltpu.CompilerParams(collective_id=0, has_side_effects=True, vmem_limit_bytes=58 * 1024 * 1024),
        cost_estimate=pl.CostEstimate(flops=3_400_000_000, bytes_accessed=6_000_000, transcendentals=2_600_000),
        name="attention_backward",
    )(offsets, queries, grad_out, key_heads.reshape(2, HALF, KVH * HD), value_heads.reshape(2, HALF, KVH * HD))
    return pl.pallas_call(
        write_kernel,
        out_shape=(dq, grads, grads),
        in_specs=[hbm, hbm],
        out_specs=(hbm, hbm, hbm),
        scratch_shapes=[vmem(queries.shape, BF16), vmem(shares.shape, BF16), vmem((2, TOK, KVH * HD), F32),
                        dma((CHUNKS + 1,)), dma((2 * CHUNKS + 1,))],
        compiler_params=pltpu.CompilerParams(vmem_limit_bytes=58 * 1024 * 1024),
        name="write_out",
    )(dq_done, shares_done)


def solution(mesh):
    in_specs = (P(None, "ctx", "kv"), P("ctx", None), P("ctx", None), P(None, "ctx", "kv"), P())
    out_specs = (P(None, "ctx", "kv"), P("ctx", None), P("ctx", None))
    return jax.shard_map(local, mesh=mesh, in_specs=in_specs, out_specs=out_specs, check_vma=False)
```

```python
import jax
import jax.numpy as jnp
from jax import lax
from jax.experimental import pallas as pl
from jax.experimental.pallas import tpu as pltpu
from jax.sharding import PartitionSpec as P

KVH = 8
HD = 128
TOK = 192
HALF = 96
CTX = 16
TOTAL = CTX * TOK
BLOCKS = 2 * CTX
LAYERS = 2
HEADS = 4
UNITS = LAYERS * HEADS
ROWS = UNITS * HALF
TILE = 384
TILE_BLOCKS = TILE // HALF
TILES = TOTAL // TILE
SLOTS = TILES + 1
SPLIT = 2
CHUNK = HALF // SPLIT
CHUNKS = 2 * SPLIT
SCALE = HD ** -0.5
EXP2_SCALE = SCALE * 1.4426950408889634
MESH = pl.DeviceIdType.MESH
BF16 = jnp.bfloat16
F32 = jnp.float32
UNROLL = 3
KEYS, VALUES = 0, 1


def ctx_of(y, z_hi, core):
    return y * 4 + z_hi * 2 + core


def head_of(z_lo, x):
    return z_lo * 2 + x // 2


def kernel(off_ref, q_ref, g_ref, k_ref, v_ref, dq_ref, out_ref,
           rank_of, block_at, stage, all_k, all_v, sorted_k, sorted_v, qs, gs, s_scr, p_scr, d_scr, k_acc, v_acc, q_acc, top_hist, sum_hist, delta_hist, stats, dq_out,
           parts, chip_in, chip_sum, y_in, y_sum, z_in, shares,
           in_sem, own_sem, cross_sem, near_sem, over_sem, mate_sem, chip_sem, y_sem, z_sem, x_sem, out_sem):
    ctx, kv = lax.axis_index("ctx"), lax.axis_index("kv")
    y, z_hi, core, z_lo, x = ctx // 4, (ctx // 2) % 2, ctx % 2, kv // 4, kv % 4
    mate = ctx_of(y, z_hi, 1 - core)
    far = ctx_of(y, 1 - z_hi, core)
    odd = x % 2
    pair = z_lo * 4 + x + 1 - 2 * odd
    y_peers = [ctx_of((y + step) % 4, z_hi, core) for step in (1, 2, 3)]
    x_peers = [z_lo * 4 + (x + step) % 4 for step in (1, 2, 3)]
    z_peers = [(z_lo + step) % 4 * 4 + x for step in (1, 2, 3)]
    at_low, at_high = z_lo == 0, z_lo == 3
    nt_dims = (((1,), (1,)), ((), ()))
    tn_dims = (((0,), (0,)), ((), ()))

    barrier = pltpu.get_barrier_semaphore()
    peers = [(far, z_idx * 4 + x) for z_idx in range(4)] + [(mate, kv)] + [(c, k) for c in y_peers for k in (kv, pair)] + [(ctx, k) for k in x_peers + z_peers]
    for peer in peers:
        pl.semaphore_signal(barrier, inc=1, device_id=peer, device_id_type=MESH)

    head = head_of(z_lo, x)

    def head_slice(part, head_idx):
        return (k_ref, v_ref)[part].at[:, :, pl.ds(pl.multiple_of(head_idx * HD, HD), HD)]

    def tokens_of(part, ctx_idx):
        return (all_k, all_v)[part].at[ctx_idx // 4, ctx_idx // 2 % 2, ctx_idx % 2]

    cross_to = [jnp.where(at_low, 2 + nth, nth) for nth in range(2)]
    staged = []
    for part in (KEYS, VALUES):
        staged.append([pltpu.make_async_copy(head_slice(part, head), tokens_of(part, ctx), own_sem.at[part, 0])])
        for nth in range(2):
            staged[part].append(pltpu.make_async_copy(head_slice(part, head_of(cross_to[nth], x)), stage.at[part, nth],
                                                      own_sem.at[part, 1 + nth]))
        for copy in staged[part]:
            copy.start()

    def rank_step(block, _):
        start = off_ref[block]
        rank = jnp.int32(0)
        for other in range(1, BLOCKS):
            rank += (start >= other * HALF).astype(jnp.int32)
        rank_of[block] = rank
        return 0

    def block_step(rank, _):
        found = jnp.int32(0)
        for block in range(1, BLOCKS):
            found += (off_ref[block] == rank * HALF).astype(jnp.int32) * block
        block_at[rank] = jnp.minimum(found, BLOCKS - 1)
        return 0

    pl.semaphore_wait(barrier, len(peers))

    def describe(src, dst, send_sem, recv_sem, ctx_idx, kv_idx):
        return pltpu.make_async_remote_copy(src_ref=src, dst_ref=dst, send_sem=send_sem, recv_sem=recv_sem,
                                            device_id=(ctx_idx, kv_idx), device_id_type=MESH)

    def remote(src, dst, sems, ctx_idx, kv_idx):
        copy = describe(src, dst, sems.at[0], sems.at[1], ctx_idx, kv_idx)
        copy.start()
        return copy

    def cross(part, act):
        @pl.when(jnp.logical_or(at_low, at_high))
        def _():
            for nth in range(2):
                act(describe(stage.at[part, nth], tokens_of(part, ctx), cross_sem.at[part, 1 + nth], cross_sem.at[part, 0],
                             far, cross_to[nth] * 4 + x))

    near, over, to_mate = {}, {}, {}

    def send_near(part):
        near[part] = [remote(tokens_of(part, ctx), tokens_of(part, ctx), near_sem.at[part, step - 1], y_peers[step - 1], kv)
                      for step in (1, 2, 3)]

    def send_over(part):
        pltpu.make_async_copy(tokens_of(part, far), tokens_of(part, far), cross_sem.at[part, 0]).wait()
        over[part] = [remote(tokens_of(part, far), tokens_of(part, far), over_sem.at[part, step - 1], y_peers[step - 1], kv)
                      for step in (1, 2, 3)]

    def send_mate(part, half):
        src = (all_k, all_v)[part].at[:, half, core]
        to_mate.setdefault(part, []).append(remote(src, src, mate_sem.at[part, len(to_mate.get(part, []))], mate, kv))

    for copy in staged[KEYS]:
        copy.wait()
    cross(KEYS, lambda copy: copy.start())
    send_near(KEYS)
    for nth, (ref, dst) in enumerate(((q_ref, qs), (g_ref, gs))):
        for half in range(2):
            for unit in range(UNITS):
                layer, head = divmod(unit, HEADS)
                pltpu.make_async_copy(
                    ref.at[layer, half * HALF:(half + 1) * HALF, head * HD:(head + 1) * HD],
                    dst.at[half, unit * HALF:(unit + 1) * HALF], in_sem.at[nth]).start()
    for copy in staged[VALUES]:
        copy.wait()
    cross(KEYS, lambda copy: copy.wait_send())
    cross(VALUES, lambda copy: copy.start())
    for copy in near[KEYS]:
        copy.wait_send()
    send_near(VALUES)
    lax.fori_loop(0, BLOCKS, block_step, 0)
    send_over(KEYS)
    for copy in near[KEYS]:
        copy.wait_recv()
    send_mate(KEYS, z_hi)
    send_over(VALUES)
    lax.fori_loop(0, BLOCKS, rank_step, 0)
    for copy in over[KEYS]:
        copy.wait_recv()
    send_mate(KEYS, 1 - z_hi)
    for copy in near[VALUES]:
        copy.wait_recv()
    send_mate(VALUES, z_hi)
    for copy in to_mate[KEYS]:
        copy.wait_recv()

    by_block = [ref.reshape(BLOCKS, HALF, HD) for ref in (all_k, all_v)]

    def sort(part):
        for rank in range(BLOCKS):
            first = rank % TILE_BLOCKS * HALF
            (sorted_k, sorted_v)[part][rank // TILE_BLOCKS, first:first + HALF] = by_block[part][block_at[rank]]

    sort(KEYS)
    pltpu.make_async_copy(qs, qs, in_sem.at[0]).wait()
    pltpu.make_async_copy(gs, gs, in_sem.at[1]).wait()

    start_0, start_1 = off_ref[2 * ctx], off_ref[2 * ctx + 1]
    count_0 = sum(((start_0 >= tile * TILE).astype(jnp.int32) for tile in range(1, TILES)), jnp.int32(1))
    count_1 = SLOTS - count_0

    def slot_of(slot):
        half = (slot >= count_0).astype(jnp.int32)
        tile = slot - count_0 * half
        return half, tile, tile, pl.ds(pl.multiple_of(slot * TILE, TILE), TILE)

    def carried(slot):
        return (slot != count_0).astype(F32)

    def fold(tile, op):
        return op(tile.reshape(TILE // 8, 8, ROWS), axis=0)

    def score_step(slot, top):
        half, tile, keys, rows = slot_of(slot)
        s = lax.dot_general(sorted_k[keys], qs[half], nt_dims, preferred_element_type=F32)
        ahead = lax.broadcasted_iota(jnp.int32, (TILE, ROWS), 0) - lax.broadcasted_iota(jnp.int32, (TILE, ROWS), 1) % HALF
        s = jnp.where(ahead <= start_0 + (start_1 - start_0) * half - tile * TILE, s, -1e30)
        s_scr[rows] = s
        keep = carried(slot)
        top = jnp.maximum(top * keep - 1e30 * (1.0 - keep), fold(s, jnp.max))
        top_hist[slot] = top
        return top

    top = lax.fori_loop(0, SLOTS - UNROLL, score_step, jnp.full((8, ROWS), -1e30, F32), unroll=UNROLL)
    for copy in over[VALUES]:
        copy.wait_recv()
    send_mate(VALUES, 1 - z_hi)
    lax.fori_loop(SLOTS - UNROLL, SLOTS, score_step, top, unroll=UNROLL)
    for half, last in enumerate((count_0 - 1, SLOTS - 1)):
        stats[half, 0] = jnp.broadcast_to(jnp.max(top_hist[last], axis=0, keepdims=True), (8, ROWS))
    for copy in to_mate[VALUES]:
        copy.wait_recv()
    sort(VALUES)

    def sum_step(slot, sums):
        half, tile, keys, rows = slot_of(slot)
        weight = jnp.exp2((s_scr[rows] - stats[half, 0][:1]) * EXP2_SCALE)
        grad_prob = lax.dot_general(sorted_v[keys], gs[half], nt_dims, preferred_element_type=F32)
        s_scr[rows] = weight
        p_scr[rows] = grad_prob
        keep = carried(slot)
        total, delta = sums[0] * keep + fold(weight, jnp.sum), sums[1] * keep + fold(weight * grad_prob, jnp.sum)
        sum_hist[slot], delta_hist[slot] = total, delta
        return total, delta

    zero = jnp.zeros((8, ROWS), F32)
    lax.fori_loop(0, SLOTS, sum_step, (zero, zero), unroll=UNROLL)
    for half, last in enumerate((count_0 - 1, SLOTS - 1)):
        inv = 1.0 / jnp.sum(sum_hist[last], axis=0, keepdims=True)
        delta = jnp.sum(delta_hist[last], axis=0, keepdims=True) * inv
        stats[half, 1] = jnp.broadcast_to(inv, (8, ROWS))
        stats[half, 2] = jnp.broadcast_to(delta, (8, ROWS))

    def value_step(slot, _):
        half, tile, keys, rows = slot_of(slot)
        prob = s_scr[rows] * stats[half, 1][:1]
        v_acc[pl.ds(slot * TILE_BLOCKS, TILE_BLOCKS)] = jnp.dot(prob.astype(BF16), gs[half], preferred_element_type=F32).reshape(TILE_BLOCKS, HALF, HD)
        return 0

    def key_step(slot, _):
        half, tile, keys, rows = slot_of(slot)
        prob = s_scr[rows] * stats[half, 1][:1]
        grad_scores = (prob * (p_scr[rows] - stats[half, 2][:1])).astype(BF16)
        d_scr[rows] = grad_scores
        k_acc[pl.ds(slot * TILE_BLOCKS, TILE_BLOCKS)] = jnp.dot(grad_scores, qs[half], preferred_element_type=F32).reshape(TILE_BLOCKS, HALF, HD)
        return 0

    def query_step(slot, _):
        half, tile, keys, rows = slot_of(slot)
        term = lax.dot_general(d_scr[rows], sorted_k[keys], tn_dims, preferred_element_type=F32)
        q_acc[slot] = term + q_acc[jnp.maximum(slot - 1, 0)] * carried(slot)
        return 0

    def by_tokens(part, acc, scale, span):
        for block in range(BLOCKS):
            rank = rank_of[block]
            in_0 = (rank < count_0 * TILE_BLOCKS).astype(jnp.int32)
            in_1 = (rank < count_1 * TILE_BLOCKS).astype(jnp.int32)
            both = (acc[rank * in_0, span] * (in_0.astype(F32) * scale)
                    + acc[(count_0 * TILE_BLOCKS + rank) * in_1, span] * (in_1.astype(F32) * scale))
            parts[part, block // 2 % 2, block // 8, block % 2, block // 4 % 2, span] = both.astype(BF16)

    chunks = {KEYS: range(SPLIT), VALUES: range(SPLIT, CHUNKS)}
    chip, along, along_z, along_x, written = {}, {}, {}, {}, []

    def rows_of(chunk):
        return slice(chunk % SPLIT * CHUNK, (chunk % SPLIT + 1) * CHUNK)

    def send_chip(part, acc, scale):
        for chunk in chunks[part]:
            by_tokens(part, acc, scale, rows_of(chunk))
            chip[chunk] = remote(parts.at[part, 1 - core, :, :, :, rows_of(chunk)], chip_in.at[chunk], chip_sem.at[chunk], mate, kv)

    def send_y(part):
        for chunk in chunks[part]:
            chip[chunk].wait_recv()
            along[chunk] = []
            for step in (2, 1, 3, 0):
                to_y = (y + step) % 4
                both = parts[part, core, to_y, :, :, rows_of(chunk)].astype(F32) + chip_in[chunk, to_y].astype(F32)
                chip_sum[chunk, step] = both.astype(BF16)
                to_ctx = y_peers[step - 1] if step else ctx
                for other in ((0, 1) if step else (1,)):
                    nth = 2 * step + other - 1
                    along[chunk].append(remote(chip_sum.at[chunk, step, 1 - odd if other else odd], y_in.at[chunk, nth],
                                               y_sem.at[chunk, nth], to_ctx, pair if other else kv))

    def send_z(part):
        for chunk in chunks[part]:
            for copy in along[chunk]:
                copy.wait_recv()
            total = chip_sum[chunk, 0, odd].astype(F32)
            for nth in range(7):
                total += y_in[chunk, nth].astype(F32)
            y_sum[chunk] = total.astype(BF16)
            along_z[chunk] = [
                remote(y_sum.at[chunk, 1 - z_hi], z_in.at[chunk, 1, z_lo], z_sem.at[chunk, 1, step], far, (z_lo + step) % 4 * 4 + x)
                for step in (0, 3, 1, 2)]
            along_z[chunk] += [
                remote(y_sum.at[chunk, z_hi], z_in.at[chunk, 0, z_lo], z_sem.at[chunk, 0, step], ctx, z_peers[step - 1])
                for step in (3, 2, 1)]
            z_in[chunk, 0, z_lo] = y_sum[chunk, z_hi]

    def send_x(part):
        for chunk in chunks[part]:
            for copy in along_z[chunk]:
                copy.wait_recv()
            shares[chunk] = (z_in[chunk, 0].astype(F32) + z_in[chunk, 1].astype(F32)).astype(BF16)
            src, dst = shares.at[chunk], out_ref.at[chunk, x]
            along_x[chunk] = [remote(src, dst, x_sem.at[chunk, step - 1], ctx, x_peers[step - 1]) for step in (2, 1, 3)]
            written.append(pltpu.make_async_copy(src, dst, out_sem.at[1 + chunk]))
            written[-1].start()

    lax.fori_loop(0, SLOTS, value_step, 0, unroll=SLOTS)
    send_chip(VALUES, v_acc, 1.0)
    lax.fori_loop(0, SLOTS, key_step, 0, unroll=UNROLL)
    send_y(VALUES)
    send_chip(KEYS, k_acc, SCALE)
    q_acc[0] = jnp.zeros((ROWS, HD), F32)
    lax.fori_loop(0, 3, query_step, 0)
    send_y(KEYS)
    lax.fori_loop(3, 7, query_step, 0)
    send_z(VALUES)
    lax.fori_loop(7, SLOTS, query_step, 0)
    for half in range(2):
        last = count_0 - 1 if half == 0 else SLOTS - 1
        for unit in range(UNITS):
            layer, head_idx = divmod(unit, HEADS)
            dq_out[layer, half * HALF:(half + 1) * HALF, head_idx * HD:(head_idx + 1) * HD] = (
                q_acc[last, unit * HALF:(unit + 1) * HALF] * SCALE).astype(BF16)
    written.append(pltpu.make_async_copy(dq_out, dq_ref, out_sem.at[0]))
    written[-1].start()
    send_z(KEYS)
    send_x(VALUES)
    send_x(KEYS)
    cross(VALUES, lambda copy: copy.wait_send())
    for copy in near[VALUES] + list(chip.values()):
        copy.wait_send()
    for group in (over, to_mate, along, along_z):
        for copies in group.values():
            for copy in copies:
                copy.wait_send()
    for copy in written:
        copy.wait()
    for part in (VALUES, KEYS):
        for chunk in chunks[part]:
            for copy in along_x[chunk]:
                copy.wait()


def write_kernel(dq_in, share_in, dq_ref, gk_ref, gv_ref, dq_buf, shares, grads, in_sem, out_sem):
    dq_load = pltpu.make_async_copy(dq_in, dq_buf, in_sem.at[CHUNKS])
    loads = [pltpu.make_async_copy(share_in.at[chunk], shares.at[chunk], in_sem.at[chunk]) for chunk in range(CHUNKS)]
    for copy in loads + [dq_load]:
        copy.start()
    stores = []

    def store(src, dst):
        stores.append(pltpu.make_async_copy(src, dst, out_sem.at[len(stores)]))
        stores[-1].start()

    for part, ref in ((KEYS, gk_ref), (VALUES, gv_ref)):
        for nth in range(SPLIT):
            chunk = part * SPLIT + nth
            loads[chunk].wait()
            for half in range(2):
                rows = slice(half * HALF + nth * CHUNK, half * HALF + (nth + 1) * CHUNK)
                for x in (half, half + 2):
                    for z_lo in range(4):
                        col = head_of(z_lo, x) * HD
                        grads[part, rows, col:col + HD] = shares[chunk, x, z_lo].astype(F32)
                store(grads.at[part, rows], ref.at[rows])
    dq_load.wait()
    store(dq_buf, dq_ref)
    for copy in stores:
        copy.wait()


def local(queries, key_heads, value_heads, grad_out, offsets):
    dma, vmem = pltpu.SemaphoreType.DMA, pltpu.VMEM
    hbm = pl.BlockSpec(memory_space=pl.ANY)
    smem = pl.BlockSpec(memory_space=pltpu.SMEM)
    grads = jax.ShapeDtypeStruct((TOK, KVH * HD), F32)
    dq = jax.ShapeDtypeStruct(queries.shape, BF16)
    shares = jax.ShapeDtypeStruct((CHUNKS, 4, 4, CHUNK, HD), BF16)
    dq_done, shares_done = pl.pallas_call(
        kernel,
        out_shape=(dq, shares),
        in_specs=[smem, hbm, hbm, hbm, hbm],
        out_specs=(hbm, hbm),
        scratch_shapes=[
            pltpu.SMEM((BLOCKS,), jnp.int32), pltpu.SMEM((BLOCKS,), jnp.int32), vmem((2, 2, 2, HALF, HD), BF16),
            vmem((4, 2, 2, 2, HALF, HD), BF16), vmem((4, 2, 2, 2, HALF, HD), BF16), vmem((TILES, TILE, HD), BF16), vmem((TILES, TILE, HD), BF16),
            vmem((2, ROWS, HD), BF16), vmem((2, ROWS, HD), BF16),
            vmem((SLOTS * TILE, ROWS), F32), vmem((SLOTS * TILE, ROWS), F32), vmem((SLOTS * TILE, ROWS), BF16),
            vmem((SLOTS * TILE_BLOCKS, HALF, HD), F32), vmem((SLOTS * TILE_BLOCKS, HALF, HD), F32), vmem((SLOTS, ROWS, HD), F32),
            vmem((SLOTS, 8, ROWS), F32), vmem((SLOTS, 8, ROWS), F32), vmem((SLOTS, 8, ROWS), F32), vmem((2, 3, 8, ROWS), F32),
            vmem((LAYERS, TOK, HEADS * HD), BF16),
            vmem((2, 2, 4, 2, 2, HALF, HD), BF16),
            vmem((CHUNKS, 4, 2, 2, CHUNK, HD), BF16), vmem((CHUNKS, 4, 2, 2, CHUNK, HD), BF16),
            vmem((CHUNKS, 7, 2, CHUNK, HD), BF16), vmem((CHUNKS, 2, CHUNK, HD), BF16),
            vmem((CHUNKS, 2, 4, CHUNK, HD), BF16), vmem((CHUNKS, 4, CHUNK, HD), BF16),
            dma((2,)), dma((2, 3)), dma((2, 3)), dma((2, 3, 2)), dma((2, 3, 2)), dma((2, 2, 2)),
            dma((CHUNKS, 2)), dma((CHUNKS, 7, 2)), dma((CHUNKS, 2, 4, 2)), dma((CHUNKS, 3, 2)), dma((1 + CHUNKS,)),
        ],
        compiler_params=pltpu.CompilerParams(collective_id=0, has_side_effects=True, vmem_limit_bytes=58 * 1024 * 1024),
        cost_estimate=pl.CostEstimate(flops=3_400_000_000, bytes_accessed=6_000_000, transcendentals=2_600_000),
        name="attention_backward",
    )(offsets, queries, grad_out, key_heads.reshape(2, HALF, KVH * HD), value_heads.reshape(2, HALF, KVH * HD))
    return pl.pallas_call(
        write_kernel,
        out_shape=(dq, grads, grads),
        in_specs=[hbm, hbm],
        out_specs=(hbm, hbm, hbm),
        scratch_shapes=[vmem(queries.shape, BF16), vmem(shares.shape, BF16), vmem((2, TOK, KVH * HD), F32),
                        dma((CHUNKS + 1,)), dma((2 * CHUNKS + 1,))],
        compiler_params=pltpu.CompilerParams(vmem_limit_bytes=58 * 1024 * 1024),
        name="write_out",
    )(dq_done, shares_done)


def solution(mesh):
    in_specs = (P(None, "ctx", "kv"), P("ctx", None), P("ctx", None), P(None, "ctx", "kv"), P())
    out_specs = (P(None, "ctx", "kv"), P("ctx", None), P("ctx", None))
    return jax.shard_map(local, mesh=mesh, in_specs=in_specs, out_specs=out_specs, check_vma=False)
```
